512 devices in a mesh: pos: 128 (over z_lo, x, y, core), mode: 4 (over z_hi).
Axes of the slice: x: 4, y: 4, z: 16 (z_hi: 4, z_lo: 4; z = z_hi * 4 + z_lo), core: 2. Of those that a mesh axis runs over, the one named last changes fastest.
Arguments:
- object_field: float32 [2, 32768, 384], P(None, 'pos'), may hold values from -6 to 6
- probe: float32 [4, 2, 256, 256], P('mode'), may hold values from -3 to 3
- offsets: int32 [1024, 2], P('pos'), may hold values from 0 to 32767, as said below
- live: int32 [1024], P('pos'), may hold values from 0 to 1, as said below
- measured: float32 [1024, 256, 256], P('pos'), may hold values from 0.1 to 10
- gaps: int32 [256, 256], replicated, may hold values 0 or 1
Outputs:
- smoothed: float32 [2, 32768, 384], P(None, 'pos')
The draws below stay inside these ranges and needn't reach their ends.
Inputs may be any that keep to these rules, and one draw needn't show every extreme that they name: `offsets`: position n's row offset lies in [(n // 8) * 256, (n // 8 + 1) * 256), its column offset in [0, 128]; on every index of pos both ends of both ranges are taken. Each index of pos holds a leading run of one to 8 live slots followed by dead ones; some index has all 8 live.
All inputs are finite; a program needn't handle non-finite values.
Results may differ from the reference program's by a relative error of at most 0.0001.
Values sent between devices are 32-bit elements; how exact they have to be, the bound alone decides.
A program may use at most 64 MiB of HBM per device.

```python
import math
import jax
import jax.numpy as jnp
from jax import lax

PATCH = 256
STRIPE = 256
WIDTH = 384
P_DEV = 8
MODES = 4
NPOS = 1024
HEIGHT = 32768


def draw_offsets(key, part):
    key = jax.random.fold_in(key, 11)
    first, second = jax.random.split(key)
    index = jnp.arange(NPOS, dtype=jnp.int32)
    slot = index % P_DEV
    owner = index // P_DEV
    local = jax.random.randint(first, (NPOS,), 0, STRIPE, dtype=jnp.int32)
    local = jnp.where(slot == 0, STRIPE - 1, jnp.where(slot == 1, 0, local))
    column = jax.random.randint(second, (NPOS,), 0, WIDTH - PATCH + 1, dtype=jnp.int32)
    column = jnp.where(slot == 0, WIDTH - PATCH, jnp.where(slot == 1, 0, column))
    return jnp.stack([owner * STRIPE + local, column], axis=1).astype(jnp.int32)


def draw_live(key, part):
    key = jax.random.fold_in(key, 23)
    first, second = jax.random.split(key)
    groups = NPOS // P_DEV
    counts = jax.random.randint(first, (groups,), 1, P_DEV + 1, dtype=jnp.int32)
    fullest = jax.random.randint(second, (), 0, groups, dtype=jnp.int32)
    counts = jnp.where(jnp.arange(groups, dtype=jnp.int32) == fullest, P_DEV, counts)
    index = jnp.arange(NPOS, dtype=jnp.int32)
    return (index % P_DEV < counts[index // P_DEV]).astype(jnp.int32)


def touch_ends(array, rng, low, top_value):
    longest = array.shape.index(max(array.shape))
    spots = []
    for shift in (0, 1):
        where = [jax.random.randint(jax.random.fold_in(rng, axis), (), 0, length) for axis, length in enumerate(array.shape)]
        where[longest] = (where[longest] + shift) % array.shape[longest]
        spots.append(tuple(where))
    return array.at[spots[0]].set(low).at[spots[1]].set(top_value)


def steps_of(key, shape, shards, smallest, top_value):
    level = 1.0
    for dim, shards_of in shards:
        heights = jax.random.uniform(jax.random.fold_in(jax.random.fold_in(key, 6), dim), (shards_of,), jnp.float32, smallest / len(shards), top_value / len(shards))
        level = level * jnp.repeat(jnp.exp(heights), shape[dim] // shards_of).reshape((-1,) + (1,) * (len(shape) - 1 - dim))
    return level


def normal_values(own_key, extent, scale, most, pieces=(), held_as=jnp.bfloat16):
    entries = jax.random.normal(own_key, extent, jnp.float32) * scale
    if len(pieces) > 0:
        entries = steps_of(own_key, extent, pieces, -0.22, 0.18) * entries
    return jnp.clip(entries, min=-most, max=most).astype(held_as)


def setup_inputs(seed: int = 0) -> dict:
    key_of = jax.random.split(jax.random.key(seed), 7)
    object_field = normal_values(key_of[0], (2, HEIGHT, WIDTH), 1.0, 6.0, ((1, 128),), jnp.float32)
    probe = normal_values(key_of[1], (MODES, 2, PATCH, PATCH), 0.5, 3.0, ((0, 4),), jnp.float32)
    offsets = draw_offsets(jax.random.fold_in(key_of[6], 71), 0)
    live = draw_live(jax.random.fold_in(key_of[6], 71), 0)
    measured = jnp.clip(jnp.exp(math.log(10.0) - 4.6051702 * jax.random.uniform(key_of[4], (NPOS, PATCH, PATCH), jnp.float32) ** steps_of(key_of[4], (NPOS, PATCH, PATCH), ((0, 128),), -0.2, 0.2)), 0.1, 10.0)
    gaps = touch_ends((jax.random.randint(key_of[5], (PATCH, PATCH), 0, 8) < 7).astype(jnp.int32), jax.random.fold_in(key_of[5], 1), 0, 1)
    return dict(object_field=object_field, probe=probe, offsets=offsets, live=live, measured=measured, gaps=gaps)


update_rate = 0.2
smooth_weight = 0.1
amplitude_floor = 0.25
gradient_soften = 0.25

def smooth(rimmed):
    grid = jnp.pad(rimmed, ((0, 0), (0, 0), (1, 1)))
    corner = grid[:, :-1, :-1]
    drow = grid[:, 1:, :-1] - corner
    dcol = grid[:, :-1, 1:] - corner
    mag = jnp.sqrt(lax.optimization_barrier(jnp.sum(drow * drow + dcol * dcol, axis=0)) + gradient_soften)
    vrow = drow / mag
    vcol = dcol / mag
    spread = vrow[:, 1:, 1:] - vrow[:, :-1, 1:] + vcol[:, 1:, 1:] - vcol[:, 1:, :-1]
    return rimmed[:, 1:-1, :] + smooth_weight * spread

def reference(object_field, probe, offsets, live, measured, gaps):
    whole = object_field[0] + 1j * object_field[1]
    padded = jnp.pad(whole, ((0, STRIPE), (0, 0)))
    probes = probe[:, 0] + 1j * probe[:, 1]
    mask = gaps.astype(jnp.float32)

    def visit(total, item):
        row, col, alive, counts = item
        patch = lax.dynamic_slice(padded, (row, col), (PATCH, PATCH))
        exits = probes * patch[None]
        spec = jnp.fft.fft2(exits, norm='ortho')
        model = lax.optimization_barrier(jnp.sum(jnp.real(spec) ** 2 + jnp.imag(spec) ** 2, axis=0))
        ratio = mask * jnp.sqrt(counts) / jnp.maximum(jnp.sqrt(model), amplitude_floor) + (1.0 - mask)
        revised = jnp.fft.ifft2(ratio[None] * spec, norm='ortho')
        change = lax.optimization_barrier(jnp.sum(jnp.conj(probes) * (revised - exits), axis=0)) * alive
        current = lax.dynamic_slice(total, (row, col), (PATCH, PATCH))
        return (lax.dynamic_update_slice(total, current + change, (row, col)), None)
    start = jnp.zeros_like(padded)
    total, _ = lax.scan(visit, start, (offsets[:, 0].astype(jnp.int32), offsets[:, 1].astype(jnp.int32), live.astype(jnp.float32), measured))
    updated = whole + update_rate * total[:HEIGHT]
    stacked = jnp.stack([jnp.real(updated), jnp.imag(updated)]).astype(object_field.dtype)
    rimmed = jnp.pad(stacked, ((0, 0), (1, 1), (0, 0)))
    return smooth(rimmed)
```

```python
import jax
import jax.numpy as jnp
import ml_dtypes
import numpy as np
from jax import lax
from jax.experimental import pallas as pl
from jax.experimental.pallas import tpu as pltpu
from jax.sharding import PartitionSpec as P

PATCH = 256
HALF = PATCH // 2
TALL = PATCH + 8
F32 = jnp.float32
BF16 = jnp.bfloat16
UPDATE_RATE = 0.2
SMOOTH_WEIGHT = 0.1
GRADIENT_SOFTEN = 0.25


def dft_tables():
    k = np.arange(HALF)
    rows = []
    for odd in (0, 1):
        angle = 2.0 * np.pi * ((k[:, None] * (2 * k[None, :] + odd)) % PATCH) / PATCH
        c, s = np.cos(angle) / 16.0, np.sin(angle) / 16.0
        w = np.block([[c, -s], [s, c]])
        for m in (w, w.T):
            hi = m.astype(ml_dtypes.bfloat16)
            lo = (m - hi.astype(np.float64)).astype(ml_dtypes.bfloat16)
            rows += [hi, lo]
    order = np.concatenate([np.arange(0, PATCH, 2), np.arange(1, PATCH, 2)])
    shuffle = np.zeros((PATCH, PATCH), ml_dtypes.bfloat16)
    shuffle[order, np.arange(PATCH)] = 1
    rows.append(shuffle)
    return np.stack(rows)


def halves(x):
    hi = x.astype(BF16)
    return hi, (x - hi.astype(F32)).astype(BF16)


def dot(a, b):
    return jnp.dot(a, b, preferred_element_type=F32)


def right(x, tab, at):
    hi, lo = halves(x)
    return dot(hi, tab[at]) + dot(hi, tab[at + 1]) + dot(lo, tab[at])


def left(tab, at, x):
    hi, lo = halves(x)
    return dot(tab[at], hi) + dot(tab[at + 1], hi) + dot(tab[at], lo)


WE, WET, WO, WOT, SHUF = 0, 2, 4, 6, 8


def forward(er, ei, tab):
    a, b = er[:, :HALF], er[:, HALF:]
    c, d = ei[:, :HALF], ei[:, HALF:]
    even = right(jnp.concatenate([a + b, c + d], 1), tab, WE)
    odd = right(jnp.concatenate([a - b, c - d], 1), tab, WO)
    yr = jnp.concatenate([even[:, :HALF], odd[:, :HALF]], 1)
    yi = jnp.concatenate([even[:, HALF:], odd[:, HALF:]], 1)
    s = jnp.concatenate([yr[:HALF] + yr[HALF:], yi[:HALF] + yi[HALF:]], 0)
    d = jnp.concatenate([yr[:HALF] - yr[HALF:], yi[:HALF] - yi[HALF:]], 0)
    return left(tab, WET, s), left(tab, WOT, d)


def inverse(te, to, tab):
    a = left(tab, WE, te)
    b = left(tab, WO, to)
    s, d = a + b, a - b
    zr = jnp.concatenate([s[:HALF], d[:HALF]], 0)
    zi = jnp.concatenate([s[HALF:], d[HALF:]], 0)
    a = right(jnp.concatenate([zr[:, :HALF], zi[:, :HALF]], 1), tab, WET)
    b = right(jnp.concatenate([zr[:, HALF:], zi[:, HALF:]], 1), tab, WOT)
    s, d = a + b, a - b
    outr = jnp.concatenate([s[:, :HALF], d[:, :HALF]], 1)
    outi = jnp.concatenate([s[:, HALF:], d[:, HALF:]], 1)
    return outr, outi


def unzip_rows(x, scr):
    scr[0] = x[:, :HALF]
    scr[1] = x[:, HALF:]
    pick = lambda at: jnp.concatenate([scr[0, pl.ds(at, HALF, 2), :], scr[1, pl.ds(at, HALF, 2), :]], 1)
    return pick(0), pick(1)


def grad_kernel(rows, cols, live, obj, halo, probe, meas, gaps, tab, acc, ext, spec, mask, scr):
    n = pl.program_id(0)
    modes = probe.shape[0]
    width = obj.shape[2]

    @pl.when(n == 0)
    def _():
        acc[...] = jnp.zeros_like(acc)
        ext[:, :PATCH] = obj[...]
        ext[:, PATCH:] = halo[...]
        even, odd = unzip_rows(dot(gaps[...].astype(F32).astype(BF16), tab[SHUF]), scr)
        mask[:HALF] = even
        mask[HALF:] = odd

    @pl.when(live[n] > 0)
    def _():
        col = cols[n]
        base = pl.multiple_of(rows[n] // 8 * 8, 8)
        down = rows[n] - base
        back = lax.rem(width - col, width)
        up = lax.rem(TALL - down, TALL)

        def cut(part):
            window = pltpu.roll(ext[part, pl.ds(base, TALL), :], back, 1)[:, :PATCH]
            return pltpu.roll(window, up, 0)[:PATCH]

        def put(part, value):
            value = jnp.concatenate([value, jnp.zeros((TALL - PATCH, PATCH), F32)], 0)
            value = pltpu.roll(value, down, 0)
            value = jnp.concatenate([value, jnp.zeros((TALL, width - PATCH), F32)], 1)
            acc[part, pl.ds(base, TALL), :] += pltpu.roll(value, col, 1)

        pr = cut(0)
        pi = cut(1)
        me = md = 0.0
        for m in range(modes):
            br, bi = probe[m, 0], probe[m, 1]
            e, o = forward(br * pr - bi * pi, br * pi + bi * pr, tab)
            spec[m, 0] = e
            spec[m, 1] = o
            me = me + (e[:HALF] * e[:HALF] + e[HALF:] * e[HALF:])
            md = md + (o[:HALF] * o[:HALF] + o[HALF:] * o[HALF:])
        root = jnp.sqrt(meas[0])
        hi, lo = halves(root)
        even, odd = unzip_rows(dot(hi, tab[SHUF]) + dot(lo, tab[SHUF]), scr)
        re = mask[:HALF] * (even * lax.rsqrt(jnp.maximum(me, 0.0625)) - 1.0)
        ro = mask[HALF:] * (odd * lax.rsqrt(jnp.maximum(md, 0.0625)) - 1.0)
        re = jnp.concatenate([re, re], 0)
        ro = jnp.concatenate([ro, ro], 0)
        gr = gi = 0.0
        for m in range(modes):
            zr, zi = inverse(spec[m, 0] * re, spec[m, 1] * ro, tab)
            br, bi = probe[m, 0], probe[m, 1]
            gr = gr + (br * zr + bi * zi)
            gi = gi + (br * zi - bi * zr)
        put(0, gr)
        put(1, gi)


def gradient(obj, halo, probe, rows, cols, live, meas, gaps):
    slots = meas.shape[0]
    stripe, width = obj.shape[1], obj.shape[2]
    tab = jnp.asarray(dft_tables())
    whole = lambda a: pl.BlockSpec(a.shape, lambda n, *_: (0,) * a.ndim)
    return pl.pallas_call(
        grad_kernel,
        out_shape=jax.ShapeDtypeStruct((2, 2 * stripe, width), F32),
        grid_spec=pltpu.PrefetchScalarGridSpec(
            num_scalar_prefetch=3,
            grid=(slots,),
            in_specs=[
                whole(obj),
                whole(halo),
                whole(probe),
                pl.BlockSpec((1, PATCH, PATCH), lambda n, *_: (n, 0, 0)),
                whole(gaps),
                whole(tab),
            ],
            out_specs=pl.BlockSpec((2, 2 * stripe, width), lambda n, *_: (0, 0, 0)),
            scratch_shapes=[
                pltpu.VMEM((2, 2 * stripe, width), F32),
                pltpu.VMEM((probe.shape[0], 2, PATCH, PATCH), F32),
                pltpu.VMEM((PATCH, PATCH), F32),
                pltpu.VMEM((2, PATCH, HALF), F32),
            ],
        ),
        compiler_params=pltpu.CompilerParams(vmem_limit_bytes=56 * 2**20),
    )(rows, cols, live, obj, halo, probe, meas, gaps, tab)


def smooth_kernel(obj, own, carried, above, below, out, grid):
    width = out.shape[2]
    rows = out.shape[1]
    grid[...] = jnp.zeros_like(grid)
    grid[:, 0:8, :width] = above[...]
    grid[:, 8 : rows + 8, :width] = obj[...] + UPDATE_RATE * (own[...] + carried[...])
    grid[:, rows + 8 : rows + 16, :width] = below[...]
    total = GRADIENT_SOFTEN
    pairs = []
    for part in (0, 1):
        u = grid[part]
        drow = pltpu.roll(u, u.shape[0] - 1, 0) - u
        dcol = pltpu.roll(u, u.shape[1] - 1, 1) - u
        total = total + drow * drow + dcol * dcol
        pairs.append((u, drow, dcol))
    inv = lax.rsqrt(total)
    for part, (u, drow, dcol) in enumerate(pairs):
        vrow, vcol = drow * inv, dcol * inv
        spread = vrow - pltpu.roll(vrow, 1, 0) + vcol - pltpu.roll(vcol, 1, 1)
        out[part] = (u + SMOOTH_WEIGHT * spread)[8 : rows + 8, :width]


def smoothed(obj, own, carried, above, below):
    rows, width = obj.shape[1:]
    return pl.pallas_call(
        smooth_kernel,
        out_shape=jax.ShapeDtypeStruct(obj.shape, F32),
        scratch_shapes=[pltpu.VMEM((2, rows + 16, width + 128), F32)],
        compiler_params=pltpu.CompilerParams(vmem_limit_bytes=40 * 2**20),
    )(obj, own, carried, above, below)


def gather_probes(probe):
    flat = probe.reshape(-1, HALF)
    count = lax.axis_size("pos")
    group = 32
    rows = flat.shape[0] // group
    mine = lax.axis_index("pos") % group
    piece = lax.dynamic_slice_in_dim(flat, mine * rows, rows, 0)
    piece = lax.all_gather(piece, "mode", axis=0)
    groups = [list(range(i, i + group)) for i in range(0, count, group)]
    pieces = lax.all_gather(piece, "pos", axis=1, axis_index_groups=groups)
    modes = lax.axis_size("mode")
    return pieces.reshape((modes,) + probe.shape[1:])


def per_device(object_field, probe, offsets, live, measured, gaps):
    stripe = object_field.shape[1]
    size = lax.axis_size("pos")
    here = lax.axis_index("pos")
    down = [(i, i + 1) for i in range(size - 1)]
    up = [(i + 1, i) for i in range(size - 1)]
    halo = lax.ppermute(object_field, "pos", up)
    probes = gather_probes(probe)
    rows = offsets[:, 0] - here * stripe
    spread = gradient(object_field, halo, probes, rows, offsets[:, 1], live, measured, gaps)
    last = object_field[:, stripe - 8 :] + UPDATE_RATE * spread[:, stripe - 8 : stripe]
    moved = lax.ppermute(jnp.concatenate([last, spread[:, stripe:]], 1), "pos", down)
    first = lax.ppermute(spread[:, :8], "pos", up)
    below = halo[:, :8] + UPDATE_RATE * (first + jnp.where(here < size - 1, spread[:, stripe : stripe + 8], 0.0))
    return smoothed(object_field, spread[:, :stripe], moved[:, 8:], moved[:, :8], below)


def solution(mesh):
    return jax.shard_map(
        per_device,
        mesh=mesh,
        in_specs=(
            P(None, "pos", None),
            P("mode", None, None, None),
            P("pos", None),
            P("pos"),
            P("pos", None, None),
            P(),
        ),
        out_specs=P(None, "pos", None),
        check_vma=False,
    )
```

```python
import jax
import jax.numpy as jnp
import ml_dtypes
import numpy as np
from jax import lax
from jax.experimental import pallas as pl
from jax.experimental.pallas import tpu as pltpu
from jax.sharding import PartitionSpec as P

PATCH = 256
HALF = PATCH // 2
TALL = PATCH + 8
F32 = jnp.float32
BF16 = jnp.bfloat16
MESH = pl.DeviceIdType.MESH
UPDATE_RATE = 0.2
SMOOTH_WEIGHT = 0.1
GRADIENT_SOFTEN = 0.25


def dft_tables():
    k = np.arange(HALF)
    rows = []
    for odd in (0, 1):
        angle = 2.0 * np.pi * ((k[:, None] * (2 * k[None, :] + odd)) % PATCH) / PATCH
        c, s = np.cos(angle) / 16.0, np.sin(angle) / 16.0
        w = np.block([[c, -s], [s, c]])
        for m in (w, w.T):
            hi = m.astype(ml_dtypes.bfloat16)
            lo = (m - hi.astype(np.float64)).astype(ml_dtypes.bfloat16)
            rows += [hi, lo]
    order = np.concatenate([np.arange(0, PATCH, 2), np.arange(1, PATCH, 2)])
    shuffle = np.zeros((PATCH, PATCH), ml_dtypes.bfloat16)
    shuffle[order, np.arange(PATCH)] = 1
    rows.append(shuffle)
    return np.stack(rows)


def halves(x):
    hi = x.astype(BF16)
    return hi, (x - hi.astype(F32)).astype(BF16)


def dot(a, b):
    return jnp.dot(a, b, preferred_element_type=F32)


def right(x, tab, at):
    hi, lo = halves(x)
    return dot(hi, tab[at]) + dot(hi, tab[at + 1]) + dot(lo, tab[at])


def left(tab, at, x):
    hi, lo = halves(x)
    return dot(tab[at], hi) + dot(tab[at + 1], hi) + dot(tab[at], lo)


WE, WET, WO, WOT, SHUF = 0, 2, 4, 6, 8


def forward(er, ei, tab):
    a, b = er[:, :HALF], er[:, HALF:]
    c, d = ei[:, :HALF], ei[:, HALF:]
    even = right(jnp.concatenate([a + b, c + d], 1), tab, WE)
    odd = right(jnp.concatenate([a - b, c - d], 1), tab, WO)
    yr = jnp.concatenate([even[:, :HALF], odd[:, :HALF]], 1)
    yi = jnp.concatenate([even[:, HALF:], odd[:, HALF:]], 1)
    s = jnp.concatenate([yr[:HALF] + yr[HALF:], yi[:HALF] + yi[HALF:]], 0)
    d = jnp.concatenate([yr[:HALF] - yr[HALF:], yi[:HALF] - yi[HALF:]], 0)
    return left(tab, WET, s), left(tab, WOT, d)


def inverse(te, to, tab):
    a = left(tab, WE, te)
    b = left(tab, WO, to)
    s, d = a + b, a - b
    zr = jnp.concatenate([s[:HALF], d[:HALF]], 0)
    zi = jnp.concatenate([s[HALF:], d[HALF:]], 0)
    a = right(jnp.concatenate([zr[:, :HALF], zi[:, :HALF]], 1), tab, WET)
    b = right(jnp.concatenate([zr[:, HALF:], zi[:, HALF:]], 1), tab, WOT)
    s, d = a + b, a - b
    outr = jnp.concatenate([s[:, :HALF], d[:, :HALF]], 1)
    outi = jnp.concatenate([s[:, HALF:], d[:, HALF:]], 1)
    return outr, outi


def unzip_rows(x, scr):
    scr[0] = x[:, :HALF]
    scr[1] = x[:, HALF:]
    pick = lambda at: jnp.concatenate([scr[0, pl.ds(at, HALF, 2), :], scr[1, pl.ds(at, HALF, 2), :]], 1)
    return pick(0), pick(1)


def grad_kernel(rows, cols, live, obj, halo, probe, others, meas, gaps, tab, acc, ext, spec, mask, scr):
    n = pl.program_id(0)
    modes = spec.shape[0]
    width = obj.shape[2]

    @pl.when(n == 0)
    def _():
        acc[...] = jnp.zeros_like(acc)
        ext[:, :PATCH] = obj[...]
        ext[:, PATCH:] = halo[...]
        even, odd = unzip_rows(dot(gaps[...].astype(F32).astype(BF16), tab[SHUF]), scr)
        mask[:HALF] = even
        mask[HALF:] = odd

    @pl.when(live[n] > 0)
    def _():
        col = cols[n]
        base = pl.multiple_of(rows[n] // 8 * 8, 8)
        down = rows[n] - base
        back = lax.rem(width - col, width)
        up = lax.rem(TALL - down, TALL)

        def cut(part):
            window = pltpu.roll(ext[part, pl.ds(base, TALL), :], back, 1)[:, :PATCH]
            return pltpu.roll(window, up, 0)[:PATCH]

        def put(part, value):
            value = jnp.concatenate([value, jnp.zeros((TALL - PATCH, PATCH), F32)], 0)
            value = pltpu.roll(value, down, 0)
            value = jnp.concatenate([value, jnp.zeros((TALL, width - PATCH), F32)], 1)
            acc[part, pl.ds(base, TALL), :] += pltpu.roll(value, col, 1)

        def illumination(m):
            return (probe[0, 0], probe[0, 1]) if m == 0 else (others[m - 1, 0], others[m - 1, 1])

        pr = cut(0)
        pi = cut(1)
        me = md = 0.0
        for m in range(modes):
            br, bi = illumination(m)
            e, o = forward(br * pr - bi * pi, br * pi + bi * pr, tab)
            spec[m, 0] = e
            spec[m, 1] = o
            me = me + (e[:HALF] * e[:HALF] + e[HALF:] * e[HALF:])
            md = md + (o[:HALF] * o[:HALF] + o[HALF:] * o[HALF:])
        root = jnp.sqrt(meas[0])
        hi, lo = halves(root)
        even, odd = unzip_rows(dot(hi, tab[SHUF]) + dot(lo, tab[SHUF]), scr)
        re = mask[:HALF] * (even * lax.rsqrt(jnp.maximum(me, 0.0625)) - 1.0)
        ro = mask[HALF:] * (odd * lax.rsqrt(jnp.maximum(md, 0.0625)) - 1.0)
        re = jnp.concatenate([re, re], 0)
        ro = jnp.concatenate([ro, ro], 0)
        gr = gi = 0.0
        for m in range(modes):
            zr, zi = inverse(spec[m, 0] * re, spec[m, 1] * ro, tab)
            br, bi = illumination(m)
            gr = gr + (br * zr + bi * zi)
            gi = gi + (br * zi - bi * zr)
        put(0, gr)
        put(1, gi)


def gradient(obj, halo, probe, others, rows, cols, live, meas, gaps):
    slots = meas.shape[0]
    stripe, width = obj.shape[1], obj.shape[2]
    tab = jnp.asarray(dft_tables())
    whole = lambda a: pl.BlockSpec(a.shape, lambda n, *_: (0,) * a.ndim)
    return pl.pallas_call(
        grad_kernel,
        out_shape=jax.ShapeDtypeStruct((2, 2 * stripe, width), F32),
        grid_spec=pltpu.PrefetchScalarGridSpec(
            num_scalar_prefetch=3,
            grid=(slots,),
            in_specs=[
                whole(obj),
                whole(halo),
                whole(probe),
                whole(others),
                pl.BlockSpec((1, PATCH, PATCH), lambda n, *_: (n, 0, 0)),
                whole(gaps),
                whole(tab),
            ],
            out_specs=pl.BlockSpec((2, 2 * stripe, width), lambda n, *_: (0, 0, 0)),
            scratch_shapes=[
                pltpu.VMEM((2, 2 * stripe, width), F32),
                pltpu.VMEM((1 + others.shape[0], 2, PATCH, PATCH), F32),
                pltpu.VMEM((PATCH, PATCH), F32),
                pltpu.VMEM((2, PATCH, HALF), F32),
            ],
        ),
        compiler_params=pltpu.CompilerParams(vmem_limit_bytes=56 * 2**20),
    )(rows, cols, live, obj, halo, probe, others, meas, gaps, tab)


def smooth_kernel(obj, own, carried, above, below, out, grid):
    width = out.shape[2]
    rows = out.shape[1]
    grid[...] = jnp.zeros_like(grid)
    grid[:, 0:8, :width] = above[...]
    grid[:, 8 : rows + 8, :width] = obj[...] + UPDATE_RATE * (own[...] + carried[...])
    grid[:, rows + 8 : rows + 16, :width] = below[...]
    total = GRADIENT_SOFTEN
    pairs = []
    for part in (0, 1):
        u = grid[part]
        drow = pltpu.roll(u, u.shape[0] - 1, 0) - u
        dcol = pltpu.roll(u, u.shape[1] - 1, 1) - u
        total = total + drow * drow + dcol * dcol
        pairs.append((u, drow, dcol))
    inv = lax.rsqrt(total)
    for part, (u, drow, dcol) in enumerate(pairs):
        vrow, vcol = drow * inv, dcol * inv
        spread = vrow - pltpu.roll(vrow, 1, 0) + vcol - pltpu.roll(vcol, 1, 1)
        out[part] = (u + SMOOTH_WEIGHT * spread)[8 : rows + 8, :width]


def smoothed(obj, own, carried, above, below):
    rows, width = obj.shape[1:]
    return pl.pallas_call(
        smooth_kernel,
        out_shape=jax.ShapeDtypeStruct(obj.shape, F32),
        scratch_shapes=[pltpu.VMEM((2, rows + 16, width + 128), F32)],
        compiler_params=pltpu.CompilerParams(vmem_limit_bytes=40 * 2**20),
    )(obj, own, carried, above, below)


PLANE = 32
CHIPS = 16


def gather_kernel(probe, obj, others, halo, zs, zr, ps, pr, cs, cr, hs, hr):
    me, mode = lax.axis_index("pos"), lax.axis_index("mode")
    size, modes = lax.axis_size("pos"), lax.axis_size("mode")
    lane = me % PLANE
    plane, core, chip = me - lane, me % 2, lane // 2
    sibling = me + 1 - 2 * core
    before, after = (me + size - 1) % size, (me + 1) % size

    def at(k):
        return ((chip + k) % CHIPS) * 2 + core

    barrier = pltpu.get_barrier_semaphore()
    peers = [(me, (mode + d) % modes) for d in range(1, modes)]
    peers += [(plane + at(k), mode) for k in range(1, CHIPS)]
    peers += [(q, mode) for q in (sibling, before, after)]
    for peer in peers:
        pl.semaphore_signal(barrier, inc=1, device_id=peer, device_id_type=MESH)
    pl.semaphore_wait(barrier, len(peers))

    def send(src, dst, s, r, peer):
        copy = pltpu.make_async_remote_copy(
            src_ref=src, dst_ref=dst, send_sem=s, recv_sem=r, device_id=peer, device_id_type=MESH
        )
        copy.start()
        return copy

    across = [
        send(probe.at[lane], others.at[modes - 1 - d, lane], zs.at[d - 1], zr.at[d - 1], (me, (mode + d) % modes))
        for d in range(1, modes)
    ]
    edge = send(obj, halo, hs, hr, (before, mode))
    for copy in across:
        copy.wait_recv()

    def block(k):
        return others.at[:, at(k)]

    spread = [
        send(block(0), block(0), ps.at[k - 1], pr.at[k - 1], (plane + at(k), mode)) for k in range(1, CHIPS)
    ]
    twin = []
    for k in range(CHIPS):
        if k > 0:
            spread[CHIPS - k - 1].wait_recv()
        twin.append(send(block(k), block(k), cs.at[k], cr.at[k], (sibling, mode)))
    for copy in twin:
        copy.wait()
    for copy in spread:
        copy.wait_send()
    for copy in across:
        copy.wait_send()
    edge.wait()


def gather(probe, obj):
    modes = lax.axis_size("mode")
    pieces = probe.reshape(PLANE, -1, PATCH)
    dma = pltpu.SemaphoreType.DMA
    others, halo = pl.pallas_call(
        gather_kernel,
        out_shape=(
            jax.ShapeDtypeStruct((modes - 1,) + pieces.shape, F32),
            jax.ShapeDtypeStruct(obj.shape, F32),
        ),
        in_specs=[pl.BlockSpec(memory_space=pl.ANY)] * 2,
        out_specs=[pl.BlockSpec(memory_space=pl.ANY)] * 2,
        scratch_shapes=[
            dma((modes - 1,)),
            dma((modes - 1,)),
            dma((CHIPS - 1,)),
            dma((CHIPS - 1,)),
            dma((CHIPS,)),
            dma((CHIPS,)),
            dma,
            dma,
        ],
        compiler_params=pltpu.CompilerParams(collective_id=0, has_side_effects=True),
    )(pieces, obj)
    return others.reshape((modes - 1,) + probe.shape[1:]), halo


def per_device(object_field, probe, offsets, live, measured, gaps):
    stripe = object_field.shape[1]
    size = lax.axis_size("pos")
    here = lax.axis_index("pos")
    down = [(i, i + 1) for i in range(size - 1)]
    up = [(i + 1, i) for i in range(size - 1)]
    others, halo = gather(probe, object_field)
    halo = jnp.where(here < size - 1, halo, 0.0)
    rows = offsets[:, 0] - here * stripe
    spread = gradient(object_field, halo, probe, others, rows, offsets[:, 1], live, measured, gaps)
    last = object_field[:, stripe - 8 :] + UPDATE_RATE * spread[:, stripe - 8 : stripe]
    moved = lax.ppermute(jnp.concatenate([last, spread[:, stripe:]], 1), "pos", down)
    first = lax.ppermute(spread[:, :8], "pos", up)
    below = halo[:, :8] + UPDATE_RATE * (first + jnp.where(here < size - 1, spread[:, stripe : stripe + 8], 0.0))
    return smoothed(object_field, spread[:, :stripe], moved[:, 8:], moved[:, :8], below)


def solution(mesh):
    return jax.shard_map(
        per_device,
        mesh=mesh,
        in_specs=(
            P(None, "pos", None),
            P("mode", None, None, None),
            P("pos", None),
            P("pos"),
            P("pos", None, None),
            P(),
        ),
        out_specs=P(None, "pos", None),
        check_vma=False,
    )
```

```python
import jax
import jax.numpy as jnp
import ml_dtypes
import numpy as np
from jax import lax
from jax.experimental import pallas as pl
from jax.experimental.pallas import tpu as pltpu
from jax.sharding import PartitionSpec as P

PATCH = 256
HALF = PATCH // 2
LANES = 128
F32 = jnp.float32
BF16 = jnp.bfloat16
MESH = pl.DeviceIdType.MESH
UPDATE_RATE = 0.2
SMOOTH_WEIGHT = 0.1
GRADIENT_SOFTEN = 0.25


def dft_tables():
    k = np.arange(HALF)
    rows = []
    for odd in (0, 1):
        angle = 2.0 * np.pi * ((k[:, None] * (2 * k[None, :] + odd)) % PATCH) / PATCH
        c, s = np.cos(angle) / 16.0, np.sin(angle) / 16.0
        w = np.block([[c, -s], [s, c]])
        for m in (w, w.T):
            hi = m.astype(ml_dtypes.bfloat16)
            lo = (m - hi.astype(np.float64)).astype(ml_dtypes.bfloat16)
            rows += [hi, lo]
    order = np.concatenate([np.arange(0, PATCH, 2), np.arange(1, PATCH, 2)])
    shuffle = np.zeros((PATCH, PATCH), ml_dtypes.bfloat16)
    shuffle[order, np.arange(PATCH)] = 1
    rows.append(shuffle)
    return np.stack(rows)


def halves(x):
    hi = x.astype(BF16)
    return hi, (x - hi.astype(F32)).astype(BF16)


def dot(a, b):
    return jnp.dot(a, b, preferred_element_type=F32)


def product(a, b, c, d):
    return dot(a, c) + dot(a, d) + dot(b, c)


def right(x, tab, at):
    hi, lo = halves(x)
    return product(hi, lo, tab[at], tab[at + 1])


def left(tab, at, x):
    hi, lo = halves(x)
    return dot(tab[at], hi) + dot(tab[at + 1], hi) + dot(tab[at], lo)


WE, WET, WO, WOT, SHUF = 0, 2, 4, 6, 8


def fold(r, i):
    even = jnp.concatenate([r[:, :HALF] + r[:, HALF:], i[:, :HALF] + i[:, HALF:]], 1)
    odd = jnp.concatenate([r[:, :HALF] - r[:, HALF:], i[:, :HALF] - i[:, HALF:]], 1)
    return even, odd


def down_columns(e, o, tab):
    yr = jnp.concatenate([e[:, :HALF], o[:, :HALF]], 1)
    yi = jnp.concatenate([e[:, HALF:], o[:, HALF:]], 1)
    s = jnp.concatenate([yr[:HALF] + yr[HALF:], yi[:HALF] + yi[HALF:]], 0)
    d = jnp.concatenate([yr[:HALF] - yr[HALF:], yi[:HALF] - yi[HALF:]], 0)
    return left(tab, WET, s), left(tab, WOT, d)


def up_columns(te, to, tab):
    a, b = left(tab, WE, te), left(tab, WO, to)
    s, d = a + b, a - b
    zr = jnp.concatenate([s[:HALF], d[:HALF]], 0)
    zi = jnp.concatenate([s[HALF:], d[HALF:]], 0)
    return jnp.concatenate([zr[:, :HALF], zi[:, :HALF]], 1), jnp.concatenate([zr[:, HALF:], zi[:, HALF:]], 1)


def unzip_rows(x, scr):
    scr[0] = x[:, :HALF]
    scr[1] = x[:, HALF:]
    pick = lambda at: jnp.concatenate([scr[0, pl.ds(at, HALF, 2), :], scr[1, pl.ds(at, HALF, 2), :]], 1)
    return pick(0), pick(1)


def grad_kernel(
    offsets, live, obj, halo, probe, others, meas, gaps, tab,
    acc, ext, probes, counts, holes, wave, spec, ratio, mask, scr, sems,
):
    slots, stripe = meas.shape[0], obj.shape[1]
    modes = spec.shape[0]
    tiles = acc.shape[1]
    here = lax.axis_index("pos")
    lane = lax.broadcasted_iota(jnp.int32, (PATCH, LANES), 1)
    pairs = [(obj.at[:, :, LANES * t : LANES * (t + 1)], ext.at[:, t, :stripe]) for t in range(tiles)]
    pairs += [(halo.at[:, :, LANES * t : LANES * (t + 1)], ext.at[:, t, stripe:]) for t in range(tiles)]
    pairs += [(probe.at[0], probes.at[0]), (others, probes.at[1:])]
    pairs += [(tab, wave), (gaps, holes), (meas, counts)]
    copies = [pltpu.make_async_copy(src, dst, sems.at[k]) for k, (src, dst) in enumerate(pairs)]
    for copy in copies:
        copy.start()
    acc[...] = jnp.zeros_like(acc)
    total = live[0]
    for k in range(1, slots):
        total = total + live[k]
    for copy in copies:
        copy.wait()

    @pl.when(here == lax.axis_size("pos") - 1)
    def _():
        ext[:, :, stripe:] = jnp.zeros((2, tiles, stripe, LANES), F32)

    even, odd = unzip_rows(dot(holes[...].astype(F32).astype(BF16), wave[SHUF]), scr)
    mask[:HALF] = even
    mask[HALF:] = odd

    def place(n):
        return offsets[0, n] - here * stripe, offsets[1, n]

    def cut(n):
        row, col = place(n)
        back = lax.rem(LANES - col, LANES)
        near = lane < LANES - col
        parts = []
        for part in (0, 1):
            turned = [pltpu.roll(ext[part, t, pl.ds(row, PATCH), :], back, 1) for t in range(tiles)]
            parts.append(
                jnp.concatenate([jnp.where(near, turned[t], turned[t + 1]) for t in range(tiles - 1)], 1)
            )
        return parts

    def put(n, values):
        row, col = place(n)
        shift = lax.rem(col, LANES)
        inside = lane >= col
        for part, value in enumerate(values):
            turned = [pltpu.roll(value[:, LANES * t : LANES * (t + 1)], shift, 1) for t in range(tiles - 1)]
            for t in range(tiles):
                own = turned[t] if t < tiles - 1 else 0.0
                before = turned[t - 1] if t > 0 else 0.0
                acc[part, t, pl.ds(row, PATCH), :] += jnp.where(inside, own, before)

    def span(m):
        return slice(PATCH * m, PATCH * (m + 1))

    def forward(n):
        pr, pi = cut(n)
        folded = []
        for m in range(modes):
            br, bi = probes[m, 0], probes[m, 1]
            folded.append(fold(br * pr - bi * pi, br * pi + bi * pr))
        even = right(jnp.concatenate([x[0] for x in folded], 0), wave, WE)
        odd = right(jnp.concatenate([x[1] for x in folded], 0), wave, WO)
        me = md = 0.0
        for m in range(modes):
            e, o = down_columns(even[span(m)], odd[span(m)], wave)
            spec[m, 0] = e
            spec[m, 1] = o
            me = me + (e[:HALF] * e[:HALF] + e[HALF:] * e[HALF:])
            md = md + (o[:HALF] * o[:HALF] + o[HALF:] * o[HALF:])
        hi, lo = halves(jnp.sqrt(counts[n]))
        even, odd = unzip_rows(dot(hi, wave[SHUF]) + dot(lo, wave[SHUF]), scr)
        ratio[:HALF] = mask[:HALF] * (even * lax.rsqrt(jnp.maximum(me, 0.0625)) - 1.0)
        ratio[HALF:] = mask[HALF:] * (odd * lax.rsqrt(jnp.maximum(md, 0.0625)) - 1.0)

    def inverse(n):
        re, ro = ratio[:HALF], ratio[HALF:]
        re = jnp.concatenate([re, re], 0)
        ro = jnp.concatenate([ro, ro], 0)
        z = [up_columns(spec[m, 0] * re, spec[m, 1] * ro, wave) for m in range(modes)]
        a = right(jnp.concatenate([x[0] for x in z], 0), wave, WET)
        b = right(jnp.concatenate([x[1] for x in z], 0), wave, WOT)
        gr = gi = 0.0
        for m in range(modes):
            s, d = a[span(m)] + b[span(m)], a[span(m)] - b[span(m)]
            zr = jnp.concatenate([s[:, :HALF], d[:, :HALF]], 1)
            zi = jnp.concatenate([s[:, HALF:], d[:, HALF:]], 1)
            br, bi = probes[m, 0], probes[m, 1]
            gr = gr + (br * zr + bi * zi)
            gi = gi + (br * zi - bi * zr)
        put(n, (gr, gi))

    def visit(n, carry):
        inverse(n)
        forward(n + 1)
        return carry

    forward(0)
    lax.fori_loop(0, total - 1, visit, 0)
    inverse(total - 1)


def gradient(obj, halo, probe, others, offsets, live, meas, gaps):
    stripe, width = obj.shape[1:]
    modes = 1 + others.shape[0]
    tiles = width // LANES
    tab = jnp.asarray(dft_tables())
    smem, hbm = pl.BlockSpec(memory_space=pltpu.SMEM), pl.BlockSpec(memory_space=pl.ANY)
    return pl.pallas_call(
        grad_kernel,
        out_shape=jax.ShapeDtypeStruct((2, tiles, 2 * stripe, LANES), F32),
        in_specs=[smem] * 2 + [hbm] * 7,
        out_specs=pl.BlockSpec(memory_space=pltpu.VMEM),
        scratch_shapes=[
            pltpu.VMEM((2, tiles, 2 * stripe, LANES), F32),
            pltpu.VMEM((modes, 2, PATCH, PATCH), F32),
            pltpu.VMEM(meas.shape, F32),
            pltpu.VMEM(gaps.shape, jnp.int32),
            pltpu.VMEM(tab.shape, BF16),
            pltpu.VMEM((modes, 2, PATCH, PATCH), F32),
            pltpu.VMEM((PATCH, PATCH), F32),
            pltpu.VMEM((PATCH, PATCH), F32),
            pltpu.VMEM((2, PATCH, HALF), F32),
            pltpu.SemaphoreType.DMA((2 * tiles + 5,)),
        ],
        compiler_params=pltpu.CompilerParams(vmem_limit_bytes=56 * 2**20),
    )(offsets.T, live, obj, halo, probe, others, meas, gaps, tab)


PLANE = 32
CHIPS = 16


def gather_kernel(probe, obj, others, halo, zs, zr, ps, pr, cs, cr, hs, hr):
    me, mode = lax.axis_index("pos"), lax.axis_index("mode")
    size, modes = lax.axis_size("pos"), lax.axis_size("mode")
    lane = me % PLANE
    plane, core, chip = me - lane, me % 2, lane // 2
    sibling = me + 1 - 2 * core
    before, after = (me + size - 1) % size, (me + 1) % size

    def at(k):
        return ((chip + k) % CHIPS) * 2 + core

    barrier = pltpu.get_barrier_semaphore()
    peers = [(me, (mode + d) % modes) for d in range(1, modes)]
    peers += [(plane + at(k), mode) for k in range(1, CHIPS)]
    peers += [(q, mode) for q in (sibling, before, after)]
    for peer in peers:
        pl.semaphore_signal(barrier, inc=1, device_id=peer, device_id_type=MESH)
    pl.semaphore_wait(barrier, len(peers))

    def send(src, dst, s, r, peer):
        copy = pltpu.make_async_remote_copy(
            src_ref=src, dst_ref=dst, send_sem=s, recv_sem=r, device_id=peer, device_id_type=MESH
        )
        copy.start()
        return copy

    across = [
        send(probe.at[lane], others.at[modes - 1 - d, lane], zs.at[d - 1], zr.at[d - 1], (me, (mode + d) % modes))
        for d in range(1, modes)
    ]
    edge = send(obj, halo, hs, hr, (before, mode))
    for copy in across:
        copy.wait_recv()

    def block(k):
        return others.at[:, at(k)]

    spread = [
        send(block(0), block(0), ps.at[k - 1], pr.at[k - 1], (plane + at(k), mode)) for k in range(1, CHIPS)
    ]
    twin = []
    for k in range(CHIPS):
        if k > 0:
            spread[CHIPS - k - 1].wait_recv()
        twin.append(send(block(k), block(k), cs.at[k], cr.at[k], (sibling, mode)))
    for copy in twin:
        copy.wait()
    for copy in spread:
        copy.wait_send()
    for copy in across:
        copy.wait_send()
    edge.wait()


def gather(probe, obj):
    modes = lax.axis_size("mode")
    pieces = probe.reshape(PLANE, -1, PATCH)
    dma = pltpu.SemaphoreType.DMA
    others, halo = pl.pallas_call(
        gather_kernel,
        out_shape=(
            jax.ShapeDtypeStruct((modes - 1,) + pieces.shape, F32),
            jax.ShapeDtypeStruct(obj.shape, F32),
        ),
        in_specs=[pl.BlockSpec(memory_space=pl.ANY)] * 2,
        out_specs=[pl.BlockSpec(memory_space=pl.ANY)] * 2,
        scratch_shapes=[
            dma((modes - 1,)),
            dma((modes - 1,)),
            dma((CHIPS - 1,)),
            dma((CHIPS - 1,)),
            dma((CHIPS,)),
            dma((CHIPS,)),
            dma,
            dma,
        ],
        compiler_params=pltpu.CompilerParams(collective_id=0, has_side_effects=True),
    )(pieces, obj)
    return others.reshape((modes - 1,) + probe.shape[1:]), halo


def tail_kernel(spread, obj, halo, out, grid, field, own, edge, landed, before, first, locals_, ss, rs):
    me, mode = lax.axis_index("pos"), lax.axis_index("mode")
    size = lax.axis_size("pos")
    rows, width = obj.shape[1:]
    previous, following = (me + size - 1) % size, (me + 1) % size
    barrier = pltpu.get_barrier_semaphore()
    for q in (previous, following):
        pl.semaphore_signal(barrier, inc=1, device_id=(q, mode), device_id_type=MESH)
    near = [
        pltpu.make_async_copy(src, dst, locals_.at[k])
        for k, (src, dst) in enumerate([(obj, field), (spread.at[:, :, : rows + 8], own), (halo.at[:, :8], edge)])
    ]
    for copy in near:
        copy.start()
    pl.semaphore_wait(barrier, 2)
    far = [
        (spread.at[:, :, rows - 8 :], landed, following),
        (obj.at[:, rows - 8 :], before, following),
        (spread.at[:, :, :8], first, previous),
    ]
    far = [
        pltpu.make_async_remote_copy(
            src_ref=src, dst_ref=dst, send_sem=ss.at[k], recv_sem=rs.at[k], device_id=(q, mode), device_id_type=MESH
        )
        for k, (src, dst, q) in enumerate(far)
    ]
    for copy in far:
        copy.start()
    for copy in near:
        copy.wait()
    grid[...] = jnp.zeros_like(grid)
    for copy in far:
        copy.wait()
    top = jnp.where(me > 0, 1.0, 0.0)
    bottom = jnp.where(me < size - 1, 1.0, 0.0)
    for k in range(width // LANES):
        at = slice(LANES * k, LANES * (k + 1))
        grid[:, 0:8, at] = top * (before[:, :, at] + UPDATE_RATE * landed[:, k, :8])
        grid[:, 8 : rows + 8, at] = field[:, :, at] + UPDATE_RATE * (own[:, k, :rows] + top * landed[:, k, 8:])
        grid[:, rows + 8 :, at] = bottom * (edge[:, :, at] + UPDATE_RATE * (first[:, k] + own[:, k, rows:]))
    total = GRADIENT_SOFTEN
    pairs = []
    for part in (0, 1):
        u = grid[part]
        drow = pltpu.roll(u, u.shape[0] - 1, 0) - u
        dcol = pltpu.roll(u, u.shape[1] - 1, 1) - u
        total = total + drow * drow + dcol * dcol
        pairs.append((u, drow, dcol))
    inv = lax.rsqrt(total)
    for part, (u, drow, dcol) in enumerate(pairs):
        vrow, vcol = drow * inv, dcol * inv
        change = vrow - pltpu.roll(vrow, 1, 0) + vcol - pltpu.roll(vcol, 1, 1)
        out[part] = (u + SMOOTH_WEIGHT * change)[8 : rows + 8, :width]


def finish(spread, obj, halo):
    rows, width = obj.shape[1:]
    tiles = width // LANES
    hbm, dma = pl.BlockSpec(memory_space=pl.ANY), pltpu.SemaphoreType.DMA
    return pl.pallas_call(
        tail_kernel,
        out_shape=jax.ShapeDtypeStruct(obj.shape, F32),
        in_specs=[hbm] * 3,
        out_specs=pl.BlockSpec(memory_space=pltpu.VMEM),
        scratch_shapes=[
            pltpu.VMEM((2, rows + 16, width + 128), F32),
            pltpu.VMEM((2, rows, width), F32),
            pltpu.VMEM((2, tiles, rows + 8, LANES), F32),
            pltpu.VMEM((2, 8, width), F32),
            pltpu.VMEM((2, tiles, rows + 8, LANES), F32),
            pltpu.VMEM((2, 8, width), F32),
            pltpu.VMEM((2, tiles, 8, LANES), F32),
            dma((3,)),
            dma((3,)),
            dma((3,)),
        ],
        compiler_params=pltpu.CompilerParams(collective_id=1, has_side_effects=True, vmem_limit_bytes=56 * 2**20),
    )(spread, obj, halo)


def per_device(object_field, probe, offsets, live, measured, gaps):
    others, halo = gather(probe, object_field)
    spread = gradient(object_field, halo, probe, others, offsets, live, measured, gaps)
    return finish(spread, object_field, halo)


def solution(mesh):
    return jax.shard_map(
        per_device,
        mesh=mesh,
        in_specs=(
            P(None, "pos", None),
            P("mode", None, None, None),
            P("pos", None),
            P("pos"),
            P("pos", None, None),
            P(),
        ),
        out_specs=P(None, "pos", None),
        check_vma=False,
    )
```

```python
import jax
import jax.numpy as jnp
import ml_dtypes
import numpy as np
from jax import lax
from jax.experimental import pallas as pl
from jax.experimental.pallas import tpu as pltpu
from jax.sharding import PartitionSpec as P

PATCH = 256
HALF = PATCH // 2
LANES = 128
F32 = jnp.float32
BF16 = jnp.bfloat16
MESH = pl.DeviceIdType.MESH
UPDATE_RATE = 0.2
SMOOTH_WEIGHT = 0.1
GRADIENT_SOFTEN = 0.25


def dft_tables():
    k = np.arange(HALF)
    rows = []
    for odd in (0, 1):
        angle = 2.0 * np.pi * ((k[:, None] * (2 * k[None, :] + odd)) % PATCH) / PATCH
        c, s = np.cos(angle) / 16.0, np.sin(angle) / 16.0
        w = np.block([[c, -s], [s, c]])
        for m in (w, w.T):
            hi = m.astype(ml_dtypes.bfloat16)
            lo = (m - hi.astype(np.float64)).astype(ml_dtypes.bfloat16)
            rows += [hi, lo]
    order = np.concatenate([np.arange(0, PATCH, 2), np.arange(1, PATCH, 2)])
    shuffle = np.zeros((PATCH, PATCH), ml_dtypes.bfloat16)
    shuffle[order, np.arange(PATCH)] = 1
    rows.append(shuffle)
    return np.stack(rows)


def halves(x):
    hi = x.astype(BF16)
    return hi, (x - hi.astype(F32)).astype(BF16)


def dot(a, b):
    return jnp.dot(a, b, preferred_element_type=F32)


def product(a, b, c, d):
    return dot(a, c) + dot(a, d) + dot(b, c)


def right(x, tab, at):
    hi, lo = halves(x)
    return product(hi, lo, tab[at], tab[at + 1])


def left(tab, at, x):
    hi, lo = halves(x)
    return dot(tab[at], hi) + dot(tab[at + 1], hi) + dot(tab[at], lo)


WE, WET, WO, WOT, SHUF = 0, 2, 4, 6, 8


def fold(r, i):
    even = jnp.concatenate([r[:, :HALF] + r[:, HALF:], i[:, :HALF] + i[:, HALF:]], 1)
    odd = jnp.concatenate([r[:, :HALF] - r[:, HALF:], i[:, :HALF] - i[:, HALF:]], 1)
    return even, odd


def down_columns(e, o, tab):
    yr = jnp.concatenate([e[:, :HALF], o[:, :HALF]], 1)
    yi = jnp.concatenate([e[:, HALF:], o[:, HALF:]], 1)
    s = jnp.concatenate([yr[:HALF] + yr[HALF:], yi[:HALF] + yi[HALF:]], 0)
    d = jnp.concatenate([yr[:HALF] - yr[HALF:], yi[:HALF] - yi[HALF:]], 0)
    return left(tab, WET, s), left(tab, WOT, d)


def up_columns(te, to, tab):
    a, b = left(tab, WE, te), left(tab, WO, to)
    s, d = a + b, a - b
    zr = jnp.concatenate([s[:HALF], d[:HALF]], 0)
    zi = jnp.concatenate([s[HALF:], d[HALF:]], 0)
    return jnp.concatenate([zr[:, :HALF], zi[:, :HALF]], 1), jnp.concatenate([zr[:, HALF:], zi[:, HALF:]], 1)


def unzip_rows(x, scr):
    scr[0] = x[:, :HALF]
    scr[1] = x[:, HALF:]
    pick = lambda at: jnp.concatenate([scr[0, pl.ds(at, HALF, 2), :], scr[1, pl.ds(at, HALF, 2), :]], 1)
    return pick(0), pick(1)


PLANE = 32
CHIPS = 16
BATCH = 4


def fused_kernel(
    offsets, live, obj, probe, meas, gaps, tab,
    out, acc, ext, probes, counts, holes, wave, patches, first, spec, ratio, mask, scr, wide,
    sems, zs, zr, ps, pr, cs, cr, hs, hr,
):
    slots, stripe = meas.shape[0], obj.shape[1]
    modes = probes.shape[0]
    tiles = ext.shape[1]
    me, mode = lax.axis_index("pos"), lax.axis_index("mode")
    size = lax.axis_size("pos")
    lane_of = me % PLANE
    plane, core, chip = me - lane_of, me % 2, lane_of // 2
    sibling = me + 1 - 2 * core
    before, after = (me + size - 1) % size, (me + 1) % size
    lane = lax.broadcasted_iota(jnp.int32, (PATCH, LANES), 1)

    def cols(t):
        return slice(LANES * t, LANES * (t + 1))

    pairs = [(tab, wave), (meas, counts), (gaps, holes), (probe, probes.at[0])]
    pairs += [(obj.at[:, :, cols(t)], ext.at[:, t, :stripe]) for t in range(tiles)]
    copies = [pltpu.make_async_copy(src, dst, sems.at[k]) for k, (src, dst) in enumerate(pairs)]
    for copy in copies:
        copy.start()

    def at(k):
        return ((chip + k) % CHIPS) * 2 + core

    barrier = pltpu.get_barrier_semaphore()
    peers = [(me, (mode + d) % modes) for d in range(1, modes)]
    peers += [(plane + at(k), mode) for k in range(1, CHIPS)]
    peers += [(q, mode) for q in (sibling, before, after)]
    for peer in peers:
        pl.semaphore_signal(barrier, inc=1, device_id=peer, device_id_type=MESH)
    pl.semaphore_wait(barrier, len(peers))

    def send(src, dst, s, r, peer):
        copy = pltpu.make_async_remote_copy(
            src_ref=src, dst_ref=dst, send_sem=s, recv_sem=r, device_id=peer, device_id_type=MESH
        )
        copy.start()
        return copy

    across = [
        send(probe.at[lane_of], probes.at[modes - d, lane_of], zs.at[d - 1], zr.at[d - 1], (me, (mode + d) % modes))
        for d in range(1, modes)
    ]
    edge = [
        send(obj.at[:, :, cols(t)], ext.at[:, t, stripe:], hs.at[t], hr.at[t], (before, mode)) for t in range(tiles)
    ]

    acc[...] = jnp.zeros_like(acc)
    wide[...] = jnp.zeros_like(wide)
    for copy in copies:
        copy.wait()
    even, odd = unzip_rows(dot(holes[...].astype(F32).astype(BF16), wave[SHUF]), scr)
    mask[:HALF] = even
    mask[HALF:] = odd

    def unzip(n, carry):
        hi, lo = halves(jnp.sqrt(counts[n]))
        even, odd = unzip_rows(dot(hi, wave[SHUF]) + dot(lo, wave[SHUF]), scr)
        counts[n, :HALF] = even
        counts[n, HALF:] = odd
        return carry

    lax.fori_loop(0, slots, unzip, 0)

    for copy in across:
        copy.wait_recv()

    def block(k):
        return probes.at[pl.ds(1, modes - 1), at(k)]

    spread = [
        send(block(0), block(0), ps.at[k - 1], pr.at[k - 1], (plane + at(k), mode)) for k in range(1, CHIPS)
    ]
    twin = [send(block(0), block(0), cs.at[0], cr.at[0], (sibling, mode))]
    for copy in edge:
        copy.wait_recv()

    @pl.when(me == size - 1)
    def _():
        ext[:, :, stripe:] = jnp.zeros((2, tiles, stripe, LANES), F32)

    def place(n):
        return lax.rem(offsets[0, n], stripe), offsets[1, n]

    def cut(n):
        row, col = place(n)
        back = lax.rem(LANES - col, LANES)
        near = lane < LANES - col
        parts = []
        for part in (0, 1):
            turned = [pltpu.roll(ext[part, t, pl.ds(row, PATCH), :], back, 1) for t in range(tiles)]
            parts.append(
                jnp.concatenate([jnp.where(near, turned[t], turned[t + 1]) for t in range(tiles - 1)], 1)
            )
        return parts

    def put(n, values):
        row, col = place(n)
        shift = lax.rem(col, LANES)
        inside = lane >= col
        for part, value in enumerate(values):
            turned = [pltpu.roll(value[:, cols(t)], shift, 1) for t in range(tiles - 1)]
            for t in range(tiles):
                own = turned[t] if t < tiles - 1 else 0.0
                left_of = turned[t - 1] if t > 0 else 0.0
                wide[part, t, stripe : stripe + PATCH] = jnp.where(inside, own, left_of)
                acc[part * tiles + t] += wide[part, t, pl.ds(stripe - row, 2 * stripe), :]

    def span(m):
        return slice(PATCH * m, PATCH * (m + 1))

    def light(m):
        half = PLANE // 2
        return probes[m, :half].reshape(PATCH, PATCH), probes[m, half:].reshape(PATCH, PATCH)

    def transformed(items):
        folded = []
        for m, (xr, xi) in items:
            br, bi = light(m)
            folded.append(fold(br * xr - bi * xi, br * xi + bi * xr))
        even = right(jnp.concatenate([x[0] for x in folded], 0), wave, WE)
        odd = right(jnp.concatenate([x[1] for x in folded], 0), wave, WO)
        return [down_columns(even[span(k)], odd[span(k)], wave) for k in range(len(folded))]

    def own(g, carry):
        taken = []
        for k in range(BATCH):
            n = g * BATCH + k
            xr, xi = cut(n)
            patches[n, 0] = xr
            patches[n, 1] = xi
            taken.append((0, (xr, xi)))
        for k, (e, o) in enumerate(transformed(taken)):
            first[g * BATCH + k, 0] = e
            first[g * BATCH + k, 1] = o
        return carry

    lax.fori_loop(0, slots // BATCH, own, 0)

    for k in range(1, CHIPS):
        spread[CHIPS - k - 1].wait_recv()
        twin.append(send(block(k), block(k), cs.at[k], cr.at[k], (sibling, mode)))
    for copy in twin:
        copy.wait_recv()

    def power(x):
        return x[:HALF] * x[:HALF] + x[HALF:] * x[HALF:]

    def forward(n):
        patch = patches[n, 0], patches[n, 1]
        me_, mo_ = power(first[n, 0]), power(first[n, 1])
        for k, (e, o) in enumerate(transformed([(m, patch) for m in range(1, modes)])):
            spec[k, 0] = e
            spec[k, 1] = o
            me_ = me_ + power(e)
            mo_ = mo_ + power(o)
        alive = jnp.where(live[n] > 0, 1.0, 0.0)
        for at_, total in ((slice(0, HALF), me_), (slice(HALF, PATCH), mo_)):
            change = counts[n, at_] * lax.rsqrt(jnp.maximum(total, 0.0625)) - 1.0
            ratio[at_] = (alive * mask[at_]) * change

    def inverse(n):
        re, ro = ratio[:HALF], ratio[HALF:]
        re = jnp.concatenate([re, re], 0)
        ro = jnp.concatenate([ro, ro], 0)
        source = [(first[n, 0], first[n, 1])] + [(spec[k, 0], spec[k, 1]) for k in range(modes - 1)]
        z = [up_columns(e * re, o * ro, wave) for e, o in source]
        a = right(jnp.concatenate([x[0] for x in z], 0), wave, WET)
        b = right(jnp.concatenate([x[1] for x in z], 0), wave, WOT)
        gr = gi = 0.0
        for m in range(modes):
            s, d = a[span(m)] + b[span(m)], a[span(m)] - b[span(m)]
            zr = jnp.concatenate([s[:, :HALF], d[:, :HALF]], 1)
            zi = jnp.concatenate([s[:, HALF:], d[:, HALF:]], 1)
            br, bi = light(m)
            gr = gr + (br * zr + bi * zi)
            gi = gi + (br * zi - bi * zr)
        put(n, (gr, gi))

    def visit(n, carry):
        inverse(n)
        forward(n + 1)
        return carry

    forward(0)
    lax.fori_loop(0, slots - 1, visit, 0)
    inverse(slots - 1)
    done = pltpu.make_async_copy(acc, out, sems.at[0])
    done.start()
    for copy in across + edge + spread + twin:
        copy.wait_send()
    done.wait()


def gradient(obj, probe, offsets, live, meas, gaps):
    stripe, width = obj.shape[1:]
    modes = lax.axis_size("mode")
    slots = meas.shape[0]
    tiles = width // LANES
    tab = jnp.asarray(dft_tables())
    pieces = probe.reshape(PLANE, -1, PATCH)
    smem, hbm = pl.BlockSpec(memory_space=pltpu.SMEM), pl.BlockSpec(memory_space=pl.ANY)
    vmem, dma = pltpu.VMEM, pltpu.SemaphoreType.DMA
    spread = pl.pallas_call(
        fused_kernel,
        out_shape=jax.ShapeDtypeStruct((2 * tiles, 2 * stripe, LANES), F32),
        in_specs=[smem] * 2 + [hbm] * 5,
        out_specs=hbm,
        scratch_shapes=[
            vmem((2 * tiles, 2 * stripe, LANES), F32),
            vmem((2, tiles, 2 * stripe, LANES), F32),
            vmem((modes,) + pieces.shape, F32),
            vmem(meas.shape, F32),
            vmem(gaps.shape, jnp.int32),
            vmem(tab.shape, BF16),
            vmem((slots, 2, PATCH, PATCH), F32),
            vmem((slots, 2, PATCH, PATCH), F32),
            vmem((modes - 1, 2, PATCH, PATCH), F32),
            vmem((PATCH, PATCH), F32),
            vmem((PATCH, PATCH), F32),
            vmem((2, PATCH, HALF), F32),
            vmem((2, tiles, 3 * stripe, LANES), F32),
            dma((4 + tiles,)),
            dma((modes - 1,)),
            dma((modes - 1,)),
            dma((CHIPS - 1,)),
            dma((CHIPS - 1,)),
            dma((CHIPS,)),
            dma((CHIPS,)),
            dma((tiles,)),
            dma((tiles,)),
        ],
        compiler_params=pltpu.CompilerParams(
            collective_id=0, has_side_effects=True, vmem_limit_bytes=60 * 2**20
        ),
    )(offsets.T, live, obj, pieces, meas, gaps, tab)
    return spread.reshape(2, tiles, 2 * stripe, LANES)


def tail_kernel(spread, obj, landed, before, first, beyond, ss, rs):
    me, mode = lax.axis_index("pos"), lax.axis_index("mode")
    size, rows = lax.axis_size("pos"), obj.shape[1]
    previous, following = (me + size - 1) % size, (me + 1) % size
    barrier = pltpu.get_barrier_semaphore()
    for q in (previous, following):
        pl.semaphore_signal(barrier, inc=1, device_id=(q, mode), device_id_type=MESH)
    pl.semaphore_wait(barrier, 2)
    far = [
        (spread.at[:, :, rows - 8 :], landed, following),
        (obj.at[:, rows - 8 :], before, following),
        (spread.at[:, :, :8], first, previous),
        (obj.at[:, :8], beyond, previous),
    ]
    far = [
        pltpu.make_async_remote_copy(
            src_ref=src, dst_ref=dst, send_sem=ss.at[k], recv_sem=rs.at[k], device_id=(q, mode), device_id_type=MESH
        )
        for k, (src, dst, q) in enumerate(far)
    ]
    for copy in far:
        copy.start()
    for copy in far:
        copy.wait()


def exchange(spread, obj):
    rows, width = obj.shape[1:]
    tiles = width // LANES
    hbm, dma = pl.BlockSpec(memory_space=pl.ANY), pltpu.SemaphoreType.DMA
    return pl.pallas_call(
        tail_kernel,
        out_shape=(
            jax.ShapeDtypeStruct((2, tiles, rows + 8, LANES), F32),
            jax.ShapeDtypeStruct((2, 8, width), F32),
            jax.ShapeDtypeStruct((2, tiles, 8, LANES), F32),
            jax.ShapeDtypeStruct((2, 8, width), F32),
        ),
        in_specs=[hbm] * 2,
        out_specs=[hbm] * 4,
        scratch_shapes=[dma((4,)), dma((4,))],
        compiler_params=pltpu.CompilerParams(collective_id=1, has_side_effects=True),
    )(spread, obj)


def smooth_kernel(spread, obj, beyond, landed_, before_, first_, out, grid, field, own, edge, landed, before, first, sems):
    rows, width = obj.shape[1:]
    me, size = lax.axis_index("pos"), lax.axis_size("pos")
    near = [
        (landed_, landed), (spread.at[:, :, : rows + 8], own), (obj, field),
        (beyond, edge), (before_, before), (first_, first),
    ]
    near = [pltpu.make_async_copy(src, dst, sems.at[k]) for k, (src, dst) in enumerate(near)]
    for copy in near:
        copy.start()
    grid[...] = jnp.zeros_like(grid)
    for copy in near:
        copy.wait()
    top = jnp.where(me > 0, 1.0, 0.0)
    bottom = jnp.where(me < size - 1, 1.0, 0.0)
    for k in range(width // LANES):
        at = slice(LANES * k, LANES * (k + 1))
        grid[:, 0:8, at] = top * (before[:, :, at] + UPDATE_RATE * landed[:, k, :8])
        grid[:, 8 : rows + 8, at] = field[:, :, at] + UPDATE_RATE * (own[:, k, :rows] + top * landed[:, k, 8:])
        grid[:, rows + 8 :, at] = bottom * (edge[:, :, at] + UPDATE_RATE * (first[:, k] + own[:, k, rows:]))
    total = GRADIENT_SOFTEN
    pairs = []
    for part in (0, 1):
        u = grid[part]
        drow = pltpu.roll(u, u.shape[0] - 1, 0) - u
        dcol = pltpu.roll(u, u.shape[1] - 1, 1) - u
        total = total + drow * drow + dcol * dcol
        pairs.append((u, drow, dcol))
    inv = lax.rsqrt(total)
    for part, (u, drow, dcol) in enumerate(pairs):
        vrow, vcol = drow * inv, dcol * inv
        change = vrow - pltpu.roll(vrow, 1, 0) + vcol - pltpu.roll(vcol, 1, 1)
        out[part] = (u + SMOOTH_WEIGHT * change)[8 : rows + 8, :width]


def finish(spread, obj):
    rows, width = obj.shape[1:]
    tiles = width // LANES
    landed, before, first, beyond = exchange(spread, obj)
    hbm = pl.BlockSpec(memory_space=pl.ANY)
    return pl.pallas_call(
        smooth_kernel,
        out_shape=jax.ShapeDtypeStruct(obj.shape, F32),
        in_specs=[hbm] * 6,
        out_specs=pl.BlockSpec(memory_space=pltpu.VMEM),
        scratch_shapes=[
            pltpu.VMEM((2, rows + 16, width + LANES), F32),
            pltpu.VMEM((2, rows, width), F32),
            pltpu.VMEM((2, tiles, rows + 8, LANES), F32),
            pltpu.VMEM((2, 8, width), F32),
            pltpu.VMEM((2, tiles, rows + 8, LANES), F32),
            pltpu.VMEM((2, 8, width), F32),
            pltpu.VMEM((2, tiles, 8, LANES), F32),
            pltpu.SemaphoreType.DMA((6,)),
        ],
        compiler_params=pltpu.CompilerParams(vmem_limit_bytes=56 * 2**20),
    )(spread, obj, beyond, landed, before, first)


def per_device(object_field, probe, offsets, live, measured, gaps):
    spread = gradient(object_field, probe, offsets, live, measured, gaps)
    return finish(spread, object_field)


def solution(mesh):
    return jax.shard_map(
        per_device,
        mesh=mesh,
        in_specs=(
            P(None, "pos", None),
            P("mode", None, None, None),
            P("pos", None),
            P("pos"),
            P("pos", None, None),
            P(),
        ),
        out_specs=P(None, "pos", None),
        check_vma=False,
    )
```

```python
import jax
import jax.numpy as jnp
import ml_dtypes
import numpy as np
from jax import lax
from jax.experimental import pallas as pl
from jax.experimental.pallas import tpu as pltpu
from jax.sharding import PartitionSpec as P

PATCH = 256
HALF = PATCH // 2
LANES = 128
F32 = jnp.float32
BF16 = jnp.bfloat16
MESH = pl.DeviceIdType.MESH
UPDATE_RATE = 0.2
SMOOTH_WEIGHT = 0.1
GRADIENT_SOFTEN = 0.25


def dft_tables():
    k = np.arange(HALF)
    rows = []
    for odd in (0, 1):
        angle = 2.0 * np.pi * ((k[:, None] * (2 * k[None, :] + odd)) % PATCH) / PATCH
        c, s = np.cos(angle) / 16.0, np.sin(angle) / 16.0
        w = np.block([[c, -s], [s, c]])
        for m in (w, w.T):
            hi = m.astype(ml_dtypes.bfloat16)
            lo = (m - hi.astype(np.float64)).astype(ml_dtypes.bfloat16)
            rows += [hi, lo]
    order = np.concatenate([np.arange(0, PATCH, 2), np.arange(1, PATCH, 2)])
    shuffle = np.zeros((PATCH, PATCH), ml_dtypes.bfloat16)
    shuffle[order, np.arange(PATCH)] = 1
    rows.append(shuffle)
    return np.stack(rows)


def halves(x):
    hi = x.astype(BF16)
    return hi, (x - hi.astype(F32)).astype(BF16)


def dot(a, b):
    return jnp.dot(a, b, preferred_element_type=F32)


def product(a, b, c, d):
    return dot(a, c) + dot(a, d) + dot(b, c)


def right(x, tab, at):
    hi, lo = halves(x)
    return product(hi, lo, tab[at], tab[at + 1])


def left(tab, at, x):
    hi, lo = halves(x)
    return dot(tab[at], hi) + dot(tab[at + 1], hi) + dot(tab[at], lo)


WE, WET, WO, WOT, SHUF = 0, 2, 4, 6, 8


def fold(r, i):
    even = jnp.concatenate([r[:, :HALF] + r[:, HALF:], i[:, :HALF] + i[:, HALF:]], 1)
    odd = jnp.concatenate([r[:, :HALF] - r[:, HALF:], i[:, :HALF] - i[:, HALF:]], 1)
    return even, odd


def down_columns(e, o, tab):
    yr = jnp.concatenate([e[:, :HALF], o[:, :HALF]], 1)
    yi = jnp.concatenate([e[:, HALF:], o[:, HALF:]], 1)
    s = jnp.concatenate([yr[:HALF] + yr[HALF:], yi[:HALF] + yi[HALF:]], 0)
    d = jnp.concatenate([yr[:HALF] - yr[HALF:], yi[:HALF] - yi[HALF:]], 0)
    return left(tab, WET, s), left(tab, WOT, d)


def up_columns(te, to, tab):
    a, b = left(tab, WE, te), left(tab, WO, to)
    s, d = a + b, a - b
    zr = jnp.concatenate([s[:HALF], d[:HALF]], 0)
    zi = jnp.concatenate([s[HALF:], d[HALF:]], 0)
    return jnp.concatenate([zr[:, :HALF], zi[:, :HALF]], 1), jnp.concatenate([zr[:, HALF:], zi[:, HALF:]], 1)


def unzip_rows(x, scr):
    scr[0] = x[:, :HALF]
    scr[1] = x[:, HALF:]
    pick = lambda at: jnp.concatenate([scr[0, pl.ds(at, HALF, 2), :], scr[1, pl.ds(at, HALF, 2), :]], 1)
    return pick(0), pick(1)


PLANE = 32
CHIPS = 16
BATCH = 4


def fused_kernel(
    offsets, live, obj, probe, meas, gaps, tab,
    base_out, landed, above, below, acc, ext, probes, counts, holes, wave, patches, first, spec, ratio, mask, scr, wide, base,
    sems, zs, zr, ps, pr, cs, cr, hs, hr, ts, tr,
):
    slots, stripe = meas.shape[0], obj.shape[1]
    modes = probes.shape[0]
    tiles = ext.shape[1]
    me, mode = lax.axis_index("pos"), lax.axis_index("mode")
    size = lax.axis_size("pos")
    lane_of = me % PLANE
    plane, core, chip = me - lane_of, me % 2, lane_of // 2
    sibling = me + 1 - 2 * core
    before, after = (me + size - 1) % size, (me + 1) % size
    lane = lax.broadcasted_iota(jnp.int32, (PATCH, LANES), 1)

    def cols(t):
        return slice(LANES * t, LANES * (t + 1))

    pairs = [(tab, wave), (meas, counts), (gaps, holes), (probe, probes.at[0])]
    pairs += [(obj.at[:, :, cols(t)], ext.at[:, t, :stripe]) for t in range(tiles)]
    copies = [pltpu.make_async_copy(src, dst, sems.at[k]) for k, (src, dst) in enumerate(pairs)]
    for copy in copies:
        copy.start()

    def at(k):
        return ((chip + k) % CHIPS) * 2 + core

    barrier = pltpu.get_barrier_semaphore()
    peers = [(me, (mode + d) % modes) for d in range(1, modes)]
    peers += [(plane + at(k), mode) for k in range(1, CHIPS)]
    peers += [(q, mode) for q in (sibling, before, after)]
    for peer in peers:
        pl.semaphore_signal(barrier, inc=1, device_id=peer, device_id_type=MESH)
    pl.semaphore_wait(barrier, len(peers))

    def send(src, dst, s, r, peer):
        copy = pltpu.make_async_remote_copy(
            src_ref=src, dst_ref=dst, send_sem=s, recv_sem=r, device_id=peer, device_id_type=MESH
        )
        copy.start()
        return copy

    across = [
        send(probe.at[lane_of], probes.at[modes - d, lane_of], zs.at[d - 1], zr.at[d - 1], (me, (mode + d) % modes))
        for d in range(1, modes)
    ]
    edge = [
        send(obj.at[:, :, cols(t)], ext.at[:, t, stripe:], hs.at[t], hr.at[t], (before, mode)) for t in range(tiles)
    ]

    acc[...] = jnp.zeros_like(acc)
    wide[...] = jnp.zeros_like(wide)
    for copy in copies:
        copy.wait()
    even, odd = unzip_rows(dot(holes[...].astype(F32).astype(BF16), wave[SHUF]), scr)
    mask[:HALF] = even
    mask[HALF:] = odd

    def unzip(n, carry):
        hi, lo = halves(jnp.sqrt(counts[n]))
        even, odd = unzip_rows(dot(hi, wave[SHUF]) + dot(lo, wave[SHUF]), scr)
        counts[n, :HALF] = even
        counts[n, HALF:] = odd
        return carry

    lax.fori_loop(0, slots, unzip, 0)

    for copy in across:
        copy.wait_recv()

    def block(k):
        return probes.at[pl.ds(1, modes - 1), at(k)]

    spread = [
        send(block(0), block(0), ps.at[k - 1], pr.at[k - 1], (plane + at(k), mode)) for k in range(1, CHIPS)
    ]
    twin = [send(block(0), block(0), cs.at[0], cr.at[0], (sibling, mode))]
    for copy in edge:
        copy.wait_recv()

    @pl.when(me == size - 1)
    def _():
        ext[:, :, stripe:] = jnp.zeros((2, tiles, stripe, LANES), F32)

    def place(n):
        return lax.rem(offsets[0, n], stripe), offsets[1, n]

    def cut(n):
        row, col = place(n)
        back = lax.rem(LANES - col, LANES)
        near = lane < LANES - col
        parts = []
        for part in (0, 1):
            turned = [pltpu.roll(ext[part, t, pl.ds(row, PATCH), :], back, 1) for t in range(tiles)]
            parts.append(
                jnp.concatenate([jnp.where(near, turned[t], turned[t + 1]) for t in range(tiles - 1)], 1)
            )
        return parts

    def put(n, values):
        row, col = place(n)
        shift = lax.rem(col, LANES)
        inside = lane >= col
        for part, value in enumerate(values):
            turned = [pltpu.roll(value[:, cols(t)], shift, 1) for t in range(tiles - 1)]
            for t in range(tiles):
                own = turned[t] if t < tiles - 1 else 0.0
                left_of = turned[t - 1] if t > 0 else 0.0
                wide[part, t, stripe : stripe + PATCH] = jnp.where(inside, own, left_of)
                acc[part * tiles + t] += wide[part, t, pl.ds(stripe - row, 2 * stripe), :]

    def span(m):
        return slice(PATCH * m, PATCH * (m + 1))

    def light(m):
        half = PLANE // 2
        return probes[m, :half].reshape(PATCH, PATCH), probes[m, half:].reshape(PATCH, PATCH)

    def transformed(items):
        folded = []
        for m, (xr, xi) in items:
            br, bi = light(m)
            folded.append(fold(br * xr - bi * xi, br * xi + bi * xr))
        even = right(jnp.concatenate([x[0] for x in folded], 0), wave, WE)
        odd = right(jnp.concatenate([x[1] for x in folded], 0), wave, WO)
        return [down_columns(even[span(k)], odd[span(k)], wave) for k in range(len(folded))]

    def own(g, carry):
        taken = []
        for k in range(BATCH):
            n = g * BATCH + k
            xr, xi = cut(n)
            patches[n, 0] = xr
            patches[n, 1] = xi
            taken.append((0, (xr, xi)))
        for k, (e, o) in enumerate(transformed(taken)):
            first[g * BATCH + k, 0] = e
            first[g * BATCH + k, 1] = o
        return carry

    lax.fori_loop(0, slots // BATCH, own, 0)

    for k in range(1, CHIPS):
        spread[CHIPS - k - 1].wait_recv()
        twin.append(send(block(k), block(k), cs.at[k], cr.at[k], (sibling, mode)))
    for copy in twin:
        copy.wait_recv()

    def power(x):
        return x[:HALF] * x[:HALF] + x[HALF:] * x[HALF:]

    def forward(n):
        patch = patches[n, 0], patches[n, 1]
        me_, mo_ = power(first[n, 0]), power(first[n, 1])
        for k, (e, o) in enumerate(transformed([(m, patch) for m in range(1, modes)])):
            spec[k, 0] = e
            spec[k, 1] = o
            me_ = me_ + power(e)
            mo_ = mo_ + power(o)
        alive = jnp.where(live[n] > 0, 1.0, 0.0)
        for at_, total in ((slice(0, HALF), me_), (slice(HALF, PATCH), mo_)):
            change = counts[n, at_] * lax.rsqrt(jnp.maximum(total, 0.0625)) - 1.0
            ratio[at_] = (alive * mask[at_]) * change

    def inverse(n):
        re, ro = ratio[:HALF], ratio[HALF:]
        re = jnp.concatenate([re, re], 0)
        ro = jnp.concatenate([ro, ro], 0)
        source = [(first[n, 0], first[n, 1])] + [(spec[k, 0], spec[k, 1]) for k in range(modes - 1)]
        z = [up_columns(e * re, o * ro, wave) for e, o in source]
        a = right(jnp.concatenate([x[0] for x in z], 0), wave, WET)
        b = right(jnp.concatenate([x[1] for x in z], 0), wave, WOT)
        gr = gi = 0.0
        for m in range(modes):
            s, d = a[span(m)] + b[span(m)], a[span(m)] - b[span(m)]
            zr = jnp.concatenate([s[:, :HALF], d[:, :HALF]], 1)
            zi = jnp.concatenate([s[:, HALF:], d[:, HALF:]], 1)
            br, bi = light(m)
            gr = gr + (br * zr + bi * zi)
            gi = gi + (br * zi - bi * zr)
        put(n, (gr, gi))

    def visit(n, carry):
        inverse(n)
        forward(n + 1)
        return carry

    forward(0)
    lax.fori_loop(0, slots - 1, visit, 0)
    inverse(slots - 1)
    tail = [send(acc.at[:, stripe:], landed, ts.at[0], tr.at[0], (after, mode))]
    tail.append(send(acc.at[:, :8], below, ts.at[1], tr.at[1], (before, mode)))
    for part in (0, 1):
        for t in range(tiles):
            at_ = part * tiles + t
            base[at_] = ext[part, t, : stripe + 8] + UPDATE_RATE * acc[at_, : stripe + 8]
    tail.append(send(base.at[:, stripe - 8 : stripe], above, ts.at[2], tr.at[2], (after, mode)))
    done = pltpu.make_async_copy(base, base_out, sems.at[0])
    done.start()
    for copy in across + edge + spread + twin:
        copy.wait_send()
    done.wait()
    for copy in tail:
        copy.wait()


def gradient(obj, probe, offsets, live, meas, gaps):
    stripe, width = obj.shape[1:]
    modes = lax.axis_size("mode")
    slots = meas.shape[0]
    tiles = width // LANES
    tab = jnp.asarray(dft_tables())
    pieces = probe.reshape(PLANE, -1, PATCH)
    smem, hbm = pl.BlockSpec(memory_space=pltpu.SMEM), pl.BlockSpec(memory_space=pl.ANY)
    vmem, dma = pltpu.VMEM, pltpu.SemaphoreType.DMA
    planes = lambda rows: jax.ShapeDtypeStruct((2 * tiles, rows, LANES), F32)
    return pl.pallas_call(
        fused_kernel,
        out_shape=(planes(stripe + 8), planes(stripe), planes(8), planes(8)),
        in_specs=[smem] * 2 + [hbm] * 5,
        out_specs=[hbm] * 4,
        scratch_shapes=[
            vmem((2 * tiles, 2 * stripe, LANES), F32),
            vmem((2, tiles, 2 * stripe, LANES), F32),
            vmem((modes,) + pieces.shape, F32),
            vmem(meas.shape, F32),
            vmem(gaps.shape, jnp.int32),
            vmem(tab.shape, BF16),
            vmem((slots, 2, PATCH, PATCH), F32),
            vmem((slots, 2, PATCH, PATCH), F32),
            vmem((modes - 1, 2, PATCH, PATCH), F32),
            vmem((PATCH, PATCH), F32),
            vmem((PATCH, PATCH), F32),
            vmem((2, PATCH, HALF), F32),
            vmem((2, tiles, 3 * stripe, LANES), F32),
            vmem((2 * tiles, stripe + 8, LANES), F32),
            dma((4 + tiles,)),
            dma((modes - 1,)),
            dma((modes - 1,)),
            dma((CHIPS - 1,)),
            dma((CHIPS - 1,)),
            dma((CHIPS,)),
            dma((CHIPS,)),
            dma((tiles,)),
            dma((tiles,)),
            dma((3,)),
            dma((3,)),
        ],
        compiler_params=pltpu.CompilerParams(
            collective_id=0, has_side_effects=True, vmem_limit_bytes=60 * 2**20
        ),
    )(offsets.T, live, obj, pieces, meas, gaps, tab)


def smooth_kernel(base_, landed_, above_, below_, out, grid, base, landed, above, below, sems):
    rows, width = out.shape[1:]
    tiles = width // LANES
    me, size = lax.axis_index("pos"), lax.axis_size("pos")
    near = [(base_, base), (landed_, landed), (above_, above), (below_, below)]
    near = [pltpu.make_async_copy(src, dst, sems.at[k]) for k, (src, dst) in enumerate(near)]
    for copy in near:
        copy.start()
    grid[:, :, width:] = jnp.zeros((2, rows + 16, LANES), F32)
    for copy in near:
        copy.wait()
    top = jnp.where(me > 0, 1.0, 0.0)
    bottom = jnp.where(me < size - 1, 1.0, 0.0)
    for part in (0, 1):
        for t in range(tiles):
            at, k = slice(LANES * t, LANES * (t + 1)), part * tiles + t
            grid[part, 0:8, at] = top * above[k]
            grid[part, 8 : rows + 8, at] = base[k, :rows] + (UPDATE_RATE * top) * landed[k]
            grid[part, rows + 8 :, at] = bottom * (base[k, rows:] + UPDATE_RATE * below[k])
    total = GRADIENT_SOFTEN
    pairs = []
    for part in (0, 1):
        u = grid[part]
        drow = pltpu.roll(u, u.shape[0] - 1, 0) - u
        dcol = pltpu.roll(u, u.shape[1] - 1, 1) - u
        total = total + drow * drow + dcol * dcol
        pairs.append((u, drow, dcol))
    inv = lax.rsqrt(total)
    for part, (u, drow, dcol) in enumerate(pairs):
        vrow, vcol = drow * inv, dcol * inv
        change = vrow - pltpu.roll(vrow, 1, 0) + vcol - pltpu.roll(vcol, 1, 1)
        out[part] = (u + SMOOTH_WEIGHT * change)[8 : rows + 8, :width]


def finish(shape, parts):
    rows, width = shape[1:]
    hbm = pl.BlockSpec(memory_space=pl.ANY)
    return pl.pallas_call(
        smooth_kernel,
        out_shape=jax.ShapeDtypeStruct(shape, F32),
        in_specs=[hbm] * 4,
        out_specs=pl.BlockSpec(memory_space=pltpu.VMEM),
        scratch_shapes=[pltpu.VMEM((2, rows + 16, width + LANES), F32)]
        + [pltpu.VMEM(x.shape, F32) for x in parts]
        + [pltpu.SemaphoreType.DMA((4,))],
        compiler_params=pltpu.CompilerParams(vmem_limit_bytes=56 * 2**20),
    )(*parts)


def per_device(object_field, probe, offsets, live, measured, gaps):
    return finish(object_field.shape, gradient(object_field, probe, offsets, live, measured, gaps))


def solution(mesh):
    return jax.shard_map(
        per_device,
        mesh=mesh,
        in_specs=(
            P(None, "pos", None),
            P("mode", None, None, None),
            P("pos", None),
            P("pos"),
            P("pos", None, None),
            P(),
        ),
        out_specs=P(None, "pos", None),
        check_vma=False,
    )
```

```python
import jax
import jax.numpy as jnp
import ml_dtypes
import numpy as np
from jax import lax
from jax.experimental import pallas as pl
from jax.experimental.pallas import tpu as pltpu
from jax.sharding import PartitionSpec as P

PATCH = 256
HALF = PATCH // 2
LANES = 128
F32 = jnp.float32
BF16 = jnp.bfloat16
MESH = pl.DeviceIdType.MESH
UPDATE_RATE = 0.2
SMOOTH_WEIGHT = 0.1
GRADIENT_SOFTEN = 0.25


def dft_tables():
    k = np.arange(HALF)
    rows = []
    for odd in (0, 1):
        angle = 2.0 * np.pi * ((k[:, None] * (2 * k[None, :] + odd)) % PATCH) / PATCH
        c, s = np.cos(angle) / 16.0, np.sin(angle) / 16.0
        w = np.block([[c, -s], [s, c]])
        for m in (w, w.T):
            hi = m.astype(ml_dtypes.bfloat16)
            lo = (m - hi.astype(np.float64)).astype(ml_dtypes.bfloat16)
            rows += [hi, lo]
    order = np.concatenate([np.arange(0, PATCH, 2), np.arange(1, PATCH, 2)])
    shuffle = np.zeros((PATCH, PATCH), ml_dtypes.bfloat16)
    shuffle[order, np.arange(PATCH)] = 1
    rows.append(shuffle)
    return np.stack(rows)


def halves(x):
    hi = x.astype(BF16)
    return hi, (x - hi.astype(F32)).astype(BF16)


def dot(a, b):
    return jnp.dot(a, b, preferred_element_type=F32)


def product(a, b, c, d):
    return dot(a, c) + dot(a, d) + dot(b, c)


def right(x, tab, at):
    hi, lo = halves(x)
    return product(hi, lo, tab[at], tab[at + 1])


def left(tab, at, x):
    hi, lo = halves(x)
    return dot(tab[at], hi) + dot(tab[at + 1], hi) + dot(tab[at], lo)


WE, WET, WO, WOT, SHUF = 0, 2, 4, 6, 8


def fold(r, i):
    even = jnp.concatenate([r[:, :HALF] + r[:, HALF:], i[:, :HALF] + i[:, HALF:]], 1)
    odd = jnp.concatenate([r[:, :HALF] - r[:, HALF:], i[:, :HALF] - i[:, HALF:]], 1)
    return even, odd


def down_columns(e, o, tab):
    yr = jnp.concatenate([e[:, :HALF], o[:, :HALF]], 1)
    yi = jnp.concatenate([e[:, HALF:], o[:, HALF:]], 1)
    s = jnp.concatenate([yr[:HALF] + yr[HALF:], yi[:HALF] + yi[HALF:]], 0)
    d = jnp.concatenate([yr[:HALF] - yr[HALF:], yi[:HALF] - yi[HALF:]], 0)
    return left(tab, WET, s), left(tab, WOT, d)


def up_columns(te, to, tab):
    a, b = left(tab, WE, te), left(tab, WO, to)
    s, d = a + b, a - b
    zr = jnp.concatenate([s[:HALF], d[:HALF]], 0)
    zi = jnp.concatenate([s[HALF:], d[HALF:]], 0)
    return jnp.concatenate([zr[:, :HALF], zi[:, :HALF]], 1), jnp.concatenate([zr[:, HALF:], zi[:, HALF:]], 1)


def unzip_rows(x, scr):
    scr[0] = x[:, :HALF]
    scr[1] = x[:, HALF:]
    pick = lambda at: jnp.concatenate([scr[0, pl.ds(at, HALF, 2), :], scr[1, pl.ds(at, HALF, 2), :]], 1)
    return pick(0), pick(1)


PLANE = 32
CHIPS = 16
BATCH = 4


def fused_kernel(
    offsets, live, obj, probe, meas, gaps, tab,
    base_out, landed, above, below, acc, ext, probes, counts, holes, wave, patches, first, spec, ratio, mask, scr, wide, base,
    sems, zs, zr, ps, pr, cs, cr, hs, hr, ts, tr,
):
    slots, stripe = meas.shape[0], obj.shape[1]
    modes = probes.shape[0]
    tiles = ext.shape[1]
    me, mode = lax.axis_index("pos"), lax.axis_index("mode")
    size = lax.axis_size("pos")
    lane_of = me % PLANE
    plane, core, chip = me - lane_of, me % 2, lane_of // 2
    sibling = me + 1 - 2 * core
    before, after = (me + size - 1) % size, (me + 1) % size
    lane = lax.broadcasted_iota(jnp.int32, (PATCH, LANES), 1)

    def cols(t):
        return slice(LANES * t, LANES * (t + 1))

    pairs = [(tab, wave), (meas, counts), (gaps, holes), (probe, probes.at[0])]
    pairs += [(obj.at[:, :, cols(t)], ext.at[:, t, :stripe]) for t in range(tiles)]
    copies = [pltpu.make_async_copy(src, dst, sems.at[k]) for k, (src, dst) in enumerate(pairs)]
    for copy in copies:
        copy.start()

    def at(k):
        return ((chip + k) % CHIPS) * 2 + core

    barrier = pltpu.get_barrier_semaphore()
    mirror = size - PLANE - plane + lane_of
    partners = [(me, (mode + 1) % modes), (me, (mode + 3) % modes), (mirror, (mode + 2) % modes)]
    peers = partners + [(plane + at(k), mode) for k in range(1, CHIPS)]
    peers += [(q, mode) for q in (sibling, before, after)]
    for peer in peers:
        pl.semaphore_signal(barrier, inc=1, device_id=peer, device_id_type=MESH)
    pl.semaphore_wait(barrier, len(peers))

    def send(src, dst, s, r, peer):
        copy = pltpu.make_async_remote_copy(
            src_ref=src, dst_ref=dst, send_sem=s, recv_sem=r, device_id=peer, device_id_type=MESH
        )
        copy.start()
        return copy

    across = [
        send(probe.at[lane_of], probes.at[k + 1, lane_of], zs.at[k], zr.at[k], peer)
        for k, peer in enumerate(partners)
    ]
    edge = [
        send(obj.at[:, :, cols(t)], ext.at[:, t, stripe:], hs.at[t], hr.at[t], (before, mode)) for t in range(tiles)
    ]

    acc[...] = jnp.zeros_like(acc)
    wide[...] = jnp.zeros_like(wide)
    for copy in copies:
        copy.wait()
    even, odd = unzip_rows(dot(holes[...].astype(F32).astype(BF16), wave[SHUF]), scr)
    mask[:HALF] = even
    mask[HALF:] = odd

    def unzip(n, carry):
        hi, lo = halves(jnp.sqrt(counts[n]))
        even, odd = unzip_rows(dot(hi, wave[SHUF]) + dot(lo, wave[SHUF]), scr)
        counts[n, :HALF] = even
        counts[n, HALF:] = odd
        return carry

    lax.fori_loop(0, slots, unzip, 0)

    for copy in across:
        copy.wait_recv()

    def block(k):
        return probes.at[pl.ds(1, modes - 1), at(k)]

    spread = [
        send(block(0), block(0), ps.at[k - 1], pr.at[k - 1], (plane + at(k), mode)) for k in range(1, CHIPS)
    ]
    twin = [send(block(0), block(0), cs.at[0], cr.at[0], (sibling, mode))]
    for copy in edge:
        copy.wait_recv()

    @pl.when(me == size - 1)
    def _():
        ext[:, :, stripe:] = jnp.zeros((2, tiles, stripe, LANES), F32)

    def place(n):
        return lax.rem(offsets[0, n], stripe), offsets[1, n]

    def cut(n):
        row, col = place(n)
        back = lax.rem(LANES - col, LANES)
        near = lane < LANES - col
        parts = []
        for part in (0, 1):
            turned = [pltpu.roll(ext[part, t, pl.ds(row, PATCH), :], back, 1) for t in range(tiles)]
            parts.append(
                jnp.concatenate([jnp.where(near, turned[t], turned[t + 1]) for t in range(tiles - 1)], 1)
            )
        return parts

    def put(n, values):
        row, col = place(n)
        shift = lax.rem(col, LANES)
        inside = lane >= col
        for part, value in enumerate(values):
            turned = [pltpu.roll(value[:, cols(t)], shift, 1) for t in range(tiles - 1)]
            for t in range(tiles):
                own = turned[t] if t < tiles - 1 else 0.0
                left_of = turned[t - 1] if t > 0 else 0.0
                wide[part, t, stripe : stripe + PATCH] = jnp.where(inside, own, left_of)
                acc[part * tiles + t] += wide[part, t, pl.ds(stripe - row, 2 * stripe), :]

    def span(m):
        return slice(PATCH * m, PATCH * (m + 1))

    def light(m):
        half = PLANE // 2
        return probes[m, :half].reshape(PATCH, PATCH), probes[m, half:].reshape(PATCH, PATCH)

    def transformed(items):
        folded = []
        for m, (xr, xi) in items:
            br, bi = light(m)
            folded.append(fold(br * xr - bi * xi, br * xi + bi * xr))
        even = right(jnp.concatenate([x[0] for x in folded], 0), wave, WE)
        odd = right(jnp.concatenate([x[1] for x in folded], 0), wave, WO)
        return [down_columns(even[span(k)], odd[span(k)], wave) for k in range(len(folded))]

    def own(g, carry):
        taken = []
        for k in range(BATCH):
            n = g * BATCH + k
            xr, xi = cut(n)
            patches[n, 0] = xr
            patches[n, 1] = xi
            taken.append((0, (xr, xi)))
        for k, (e, o) in enumerate(transformed(taken)):
            first[g * BATCH + k, 0] = e
            first[g * BATCH + k, 1] = o
        return carry

    own(0, 0)

    for k in range(1, CHIPS):
        spread[CHIPS - k - 1].wait_recv()
        twin.append(send(block(k), block(k), cs.at[k], cr.at[k], (sibling, mode)))
    for g in range(1, slots // BATCH):
        own(g, 0)
    for copy in twin:
        copy.wait_recv()

    def power(x):
        return x[:HALF] * x[:HALF] + x[HALF:] * x[HALF:]

    def forward(n):
        patch = patches[n, 0], patches[n, 1]
        me_, mo_ = power(first[n, 0]), power(first[n, 1])
        for k, (e, o) in enumerate(transformed([(m, patch) for m in range(1, modes)])):
            spec[k, 0] = e
            spec[k, 1] = o
            me_ = me_ + power(e)
            mo_ = mo_ + power(o)
        alive = jnp.where(live[n] > 0, 1.0, 0.0)
        for at_, total in ((slice(0, HALF), me_), (slice(HALF, PATCH), mo_)):
            change = counts[n, at_] * lax.rsqrt(jnp.maximum(total, 0.0625)) - 1.0
            ratio[at_] = (alive * mask[at_]) * change

    def inverse(n):
        re, ro = ratio[:HALF], ratio[HALF:]
        re = jnp.concatenate([re, re], 0)
        ro = jnp.concatenate([ro, ro], 0)
        source = [(first[n, 0], first[n, 1])] + [(spec[k, 0], spec[k, 1]) for k in range(modes - 1)]
        z = [up_columns(e * re, o * ro, wave) for e, o in source]
        a = right(jnp.concatenate([x[0] for x in z], 0), wave, WET)
        b = right(jnp.concatenate([x[1] for x in z], 0), wave, WOT)
        gr = gi = 0.0
        for m in range(modes):
            s, d = a[span(m)] + b[span(m)], a[span(m)] - b[span(m)]
            zr = jnp.concatenate([s[:, :HALF], d[:, :HALF]], 1)
            zi = jnp.concatenate([s[:, HALF:], d[:, HALF:]], 1)
            br, bi = light(m)
            gr = gr + (br * zr + bi * zi)
            gi = gi + (br * zi - bi * zr)
        put(n, (gr, gi))

    def visit(n, carry):
        inverse(n)
        forward(n + 1)
        return carry

    forward(0)
    lax.fori_loop(0, slots - 1, visit, 0)
    inverse(slots - 1)
    tail = [send(acc.at[:, stripe:], landed, ts.at[0], tr.at[0], (after, mode))]
    tail.append(send(acc.at[:, :8], below, ts.at[1], tr.at[1], (before, mode)))
    for part in (0, 1):
        for t in range(tiles):
            at_ = part * tiles + t
            base[at_] = ext[part, t, : stripe + 8] + UPDATE_RATE * acc[at_, : stripe + 8]
    tail.append(send(base.at[:, stripe - 8 : stripe], above, ts.at[2], tr.at[2], (after, mode)))
    done = pltpu.make_async_copy(base, base_out, sems.at[0])
    done.start()
    for copy in across + edge + spread + twin:
        copy.wait_send()
    done.wait()
    for copy in tail:
        copy.wait()


def gradient(obj, probe, offsets, live, meas, gaps):
    stripe, width = obj.shape[1:]
    modes = lax.axis_size("mode")
    slots = meas.shape[0]
    tiles = width // LANES
    tab = jnp.asarray(dft_tables())
    pieces = probe.reshape(PLANE, -1, PATCH)
    smem, hbm = pl.BlockSpec(memory_space=pltpu.SMEM), pl.BlockSpec(memory_space=pl.ANY)
    vmem, dma = pltpu.VMEM, pltpu.SemaphoreType.DMA
    planes = lambda rows: jax.ShapeDtypeStruct((2 * tiles, rows, LANES), F32)
    return pl.pallas_call(
        fused_kernel,
        out_shape=(planes(stripe + 8), planes(stripe), planes(8), planes(8)),
        in_specs=[smem] * 2 + [hbm] * 5,
        out_specs=[hbm] * 4,
        scratch_shapes=[
            vmem((2 * tiles, 2 * stripe, LANES), F32),
            vmem((2, tiles, 2 * stripe, LANES), F32),
            vmem((modes,) + pieces.shape, F32),
            vmem(meas.shape, F32),
            vmem(gaps.shape, jnp.int32),
            vmem(tab.shape, BF16),
            vmem((slots, 2, PATCH, PATCH), F32),
            vmem((slots, 2, PATCH, PATCH), F32),
            vmem((modes - 1, 2, PATCH, PATCH), F32),
            vmem((PATCH, PATCH), F32),
            vmem((PATCH, PATCH), F32),
            vmem((2, PATCH, HALF), F32),
            vmem((2, tiles, 3 * stripe, LANES), F32),
            vmem((2 * tiles, stripe + 8, LANES), F32),
            dma((4 + tiles,)),
            dma((modes - 1,)),
            dma((modes - 1,)),
            dma((CHIPS - 1,)),
            dma((CHIPS - 1,)),
            dma((CHIPS,)),
            dma((CHIPS,)),
            dma((tiles,)),
            dma((tiles,)),
            dma((3,)),
            dma((3,)),
        ],
        compiler_params=pltpu.CompilerParams(
            collective_id=0, has_side_effects=True, vmem_limit_bytes=60 * 2**20
        ),
    )(offsets.T, live, obj, pieces, meas, gaps, tab)


def smooth_kernel(base_, landed_, above_, below_, result, out, grid, base, landed, above, below, sems):
    rows, width = out.shape[1:]
    tiles = width // LANES
    me, size = lax.axis_index("pos"), lax.axis_size("pos")
    near = [(base_, base), (landed_, landed), (above_, above), (below_, below)]
    near = [pltpu.make_async_copy(src, dst, sems.at[k]) for k, (src, dst) in enumerate(near)]
    for copy in near:
        copy.start()
    grid[:, :, width:] = jnp.zeros((2, rows + 16, LANES), F32)
    for copy in near:
        copy.wait()
    top = jnp.where(me > 0, 1.0, 0.0)
    bottom = jnp.where(me < size - 1, 1.0, 0.0)
    for part in (0, 1):
        for t in range(tiles):
            at, k = slice(LANES * t, LANES * (t + 1)), part * tiles + t
            grid[part, 0:8, at] = top * above[k]
            grid[part, 8 : rows + 8, at] = base[k, :rows] + (UPDATE_RATE * top) * landed[k]
            grid[part, rows + 8 :, at] = bottom * (base[k, rows:] + UPDATE_RATE * below[k])
    total = GRADIENT_SOFTEN
    pairs = []
    for part in (0, 1):
        u = grid[part]
        drow = pltpu.roll(u, u.shape[0] - 1, 0) - u
        dcol = pltpu.roll(u, u.shape[1] - 1, 1) - u
        total = total + drow * drow + dcol * dcol
        pairs.append((u, drow, dcol))
    inv = lax.rsqrt(total)
    leaving = []
    for part, (u, drow, dcol) in enumerate(pairs):
        vrow, vcol = drow * inv, dcol * inv
        change = vrow - pltpu.roll(vrow, 1, 0) + vcol - pltpu.roll(vcol, 1, 1)
        out[part] = (u + SMOOTH_WEIGHT * change)[8 : rows + 8, :width]
        leaving.append(pltpu.make_async_copy(out.at[part], result.at[part], sems.at[part]))
        leaving[part].start()
    for copy in leaving:
        copy.wait()


def finish(shape, parts):
    rows, width = shape[1:]
    hbm = pl.BlockSpec(memory_space=pl.ANY)
    return pl.pallas_call(
        smooth_kernel,
        out_shape=jax.ShapeDtypeStruct(shape, F32),
        in_specs=[hbm] * 4,
        out_specs=hbm,
        scratch_shapes=[pltpu.VMEM(shape, F32), pltpu.VMEM((2, rows + 16, width + LANES), F32)]
        + [pltpu.VMEM(x.shape, F32) for x in parts]
        + [pltpu.SemaphoreType.DMA((4,))],
        compiler_params=pltpu.CompilerParams(vmem_limit_bytes=56 * 2**20),
    )(*parts)


def per_device(object_field, probe, offsets, live, measured, gaps):
    return finish(object_field.shape, gradient(object_field, probe, offsets, live, measured, gaps))


def solution(mesh):
    return jax.shard_map(
        per_device,
        mesh=mesh,
        in_specs=(
            P(None, "pos", None),
            P("mode", None, None, None),
            P("pos", None),
            P("pos"),
            P("pos", None, None),
            P(),
        ),
        out_specs=P(None, "pos", None),
        check_vma=False,
    )
```
